32 devices in a mesh: rep: 8 (over y, x, core), blk: 4 (over z).
Axes of the slice: x: 2, y: 2, z: 4, core: 2. Of those that a mesh axis runs over, the one named last changes fastest.
Arguments:
- tokens: bfloat16 [4096, 1536], P(('rep', 'blk')), may hold values from -64 to 64
- attn_in: float32 [1536, 2048], P(('rep', 'blk')), may hold values from -8 to 8
- attn_out: float32 [1536, 1536], P(('rep', 'blk')), may hold values from -0.15625 to 0.15625
- expert_in: float32 [16, 1536, 1536], P(None, ('rep', 'blk')), may hold values from -0.15625 to 0.15625
- expert_out: float32 [16, 768, 1536], P(None, ('rep', 'blk')), may hold values from -0.21875 to 0.21875
- attn_gain: float32 [1536], replicated, may hold values from 0.25 to 1.75
- moe_gain: float32 [1536], replicated, may hold values from 0.25 to 1.75
- lengths: int32 [8, 6], P('rep'), may hold values from 1 to 256, 512 in all within a row
- page_table: int32 [8, 4], P('rep'), may hold values from 0 to 3, each once within a row
- routes: int32 [4096, 4], P(('rep', 'blk')), may hold values from 0 to 15, all different within a row; in each aligned block of 128 rows (0 to 127, 128 to 255, ...) at most 64 rows name the same one
- gates: bfloat16 [4096, 4], P(('rep', 'blk')), may hold values from 0.19921875 to 1
Outputs:
- mixed: bfloat16 [4096, 1536], P(('rep', 'blk'))
- kv_cache: bfloat16 [32, 128, 512], P(('rep', 'blk'))
The draws below stay inside these ranges and needn't reach their ends.
Inputs may be any that keep to these rules, and one draw needn't show every extreme that they name: Each replica's lengths sum to 512. `page_table`: each replica's row is a permutation of its 4 pages. `routes`: a token names 4 different experts; among the rows of one device no expert is named more than 64 times.
All inputs are finite; a program needn't handle non-finite values.
Results may differ from the reference program's by a relative error of at most 0.013.
Values may be sent and summed in bfloat16 or wider, within the bound.
No kernel may reach another device: no remote copies, remote signals or barrier semaphores. Data moves between devices by JAX's collectives and lax.ppermute only.
A program may use at most 128 MiB of HBM per device.

```python
import math
import jax
import jax.numpy as jnp
import numpy as np
from jax import lax

D = 1536
FF = 768
QH = 12
KVH = 2
HD = 128
TOP = 4
E = 16
PAGE = 128
SEQS = 6
TOK_DEV = 128
GROUP = 512
TOKENS = 4096
PAGES = 4
MAXLEN = 256
CAP = 64
QW = 1536
KVW = 512
QKV = 2048
N_REP = 8
N_BLK = 4


def draw_tokens(key, part):
    first = jax.random.fold_in(key, 0)
    values = jax.random.truncated_normal(first, -6.0, 6.0, (TOKENS, D), jnp.float32)
    return values.astype(jnp.bfloat16)


def draw_attn_in(key, part):
    first = jax.random.fold_in(key, 0)
    base = jax.random.truncated_normal(first, -6.0, 6.0, (D, QKV), jnp.float32) / jnp.sqrt(jnp.float32(D))
    return jnp.clip(base, -8.0, 8.0)


def level_of(own_key, shape, cuts, smallest, high):
    loudness, own = 1.0, jax.random.fold_in(own_key, 6)
    for dim, shards_of in cuts:
        draws = jnp.exp(jax.random.uniform(jax.random.fold_in(own, dim), (shards_of,), jnp.float32, smallest / len(cuts), high / len(cuts)))
        loudness = loudness * jnp.repeat(draws, shape[dim] // shards_of).reshape([-1 if axis == dim else 1 for axis in range(len(shape))])
    return loudness


def length_profile(count, total, limit, slope):
    loads = [(1 << 20) // math.isqrt(grade ** slope) + 1 for grade in range(2, count + 1)]
    rest, counts = total - limit - (count - 1), [1] * (count - 1)
    while rest > 0:
        free = [i for i in range(count - 1) if counts[i] < limit]
        mass, left = sum([loads[i] for i in free]), rest
        for i in free:
            addition = min(limit - counts[i], max(1, left * loads[i] // mass), rest)
            counts[i] = counts[i] + addition
            rest = rest - addition
    return np.array([limit] + counts)


def ragged_sizes(own_key, number_of, total, reach, skew):
    if number_of == 2:
        one = jax.random.randint(own_key, (), max(1, total - reach), min(reach, total - 1) + 1)
        return jnp.stack([one, total - one])
    sizes = jnp.asarray(length_profile(number_of, total, reach, skew), jnp.int32)
    twos = (number_of - 1) // 2
    donor, taker = sizes[1:1 + 2 * twos:2], sizes[2:2 + 2 * twos:2]
    slack = jnp.minimum(donor - 1, reach - taker)
    moved = jax.random.randint(jax.random.fold_in(own_key, 1), (twos,), 0, 1 << 20) % (slack + 1)
    sizes = sizes.at[1:1 + 2 * twos:2].set(donor - moved).at[2:2 + 2 * twos:2].set(taker + moved)
    return sizes[jax.random.permutation(jax.random.fold_in(own_key, 2), number_of)]


def routed_block(stream_key, own, number, rows, amount, top, limit, slope):
    order = jax.random.permutation(stream_key, amount)
    crowded, ordinary = shares(amount, rows * top, limit, slope, True), shares(amount, rows * top, limit, slope, False)
    places = jnp.arange(amount)

    def named(tallies, rotation):
        used = int((tallies > 0).sum())
        fixed = max(1, used // 4)
        shifted = fixed + (places - fixed + rotation * (used - fixed)) % max(1, amount - fixed)
        return jnp.zeros((amount,), jnp.int32).at[order[jnp.where(places < fixed, places, shifted)]].set(jnp.asarray(tallies, jnp.int32))

    tallies = jnp.where(number % 4 == 0, named(crowded, number // 4), named(ordinary, number - number // 4 - 1))
    mixed = jax.random.permutation(jax.random.fold_in(own, 3), amount)
    donor, receiver = mixed[0:amount // 2 * 2:2], mixed[1:amount // 2 * 2:2]
    margin = jnp.minimum(tallies[donor] - 1, limit - tallies[receiver]) // 2
    margin = jnp.where((donor == order[0]) | (receiver == order[0]) | (tallies[receiver] == 0), 0, jnp.maximum(margin, 0))
    shifted = jax.random.randint(jax.random.fold_in(own, 4), (amount // 2,), 0, 1 << 20) % (margin + 1)
    tallies = tallies.at[donor].add(-shifted).at[receiver].add(shifted)
    members = jnp.searchsorted(jnp.cumsum(tallies), jnp.arange(rows * top), side="right").astype(jnp.int32)
    grid = members.reshape(top, rows).T
    grid = grid[jax.random.permutation(jax.random.fold_in(own, 1), rows)]
    rotation = jax.random.randint(jax.random.fold_in(own, 2), (rows, 1), 0, top)
    return jnp.take_along_axis(grid, (jnp.arange(top)[None, :] + rotation) % top, axis=1)


def shares(amount, total, bound, skew, full):
    weights = [(1 << 20) // math.isqrt(rank ** skew) + 1 for rank in range(1, amount + 1)]
    largest = bound if full else min(bound, max(-(-total // amount), total * weights[0] // sum(weights)))
    least = 1 if total - largest >= amount - 1 else 0
    holding, rest = [largest] + [least] * (amount - 1), total - largest - least * (amount - 1)
    while rest > 0:
        candidates = [i for i in range(1, amount) if holding[i] < largest] or [i for i in range(1, amount) if holding[i] < bound]
        pool, left = sum([weights[i] for i in candidates]), rest
        for i in candidates:
            more = min(bound - holding[i], max(1, left * weights[i] // pool), rest)
            holding[i] = holding[i] + more
            rest = rest - more
    return np.array(holding)


def gaussian(own_key, dims, width, limit, pieces=(), kind=jnp.bfloat16):
    values = jax.random.normal(own_key, dims, jnp.float32) * width
    if len(pieces) > 0:
        values = level_of(own_key, dims, pieces, -0.22, 0.18) * values
    return jnp.clip(values, min=-limit, max=limit).astype(kind)


def setup_inputs(seed: int = 0) -> dict:
    splits = jax.random.split(jax.random.key(seed), 12)
    tokens = draw_tokens(jax.random.fold_in(splits[11], 71), 0)
    attn_in = draw_attn_in(jax.random.fold_in(splits[11], 71), 0)
    attn_out = gaussian(splits[2], (QW, D), QW ** -0.5, 0.15625, ((0, 32),), jnp.float32)
    expert_in = gaussian(splits[3], (E, D, 2 * FF), D ** -0.5, 0.15625, ((1, 32),), jnp.float32)
    expert_out = gaussian(splits[4], (E, FF, D), FF ** -0.5, 0.21875, ((1, 32),), jnp.float32)
    attn_gain = jnp.clip(1.0 + 0.15 * jax.random.normal(splits[5], (D,), jnp.float32), 0.25, 1.75)
    moe_gain = jnp.clip(1.0 + 0.15 * jax.random.normal(splits[6], (D,), jnp.float32), 0.25, 1.75)
    lengths = jax.vmap(lambda own: ragged_sizes(own, SEQS, GROUP, MAXLEN, 2))(jax.random.split(splits[7], N_REP)).reshape((N_REP, SEQS)).astype(jnp.int32)
    page_table = jax.vmap(lambda own: jax.random.permutation(own, PAGES))(jax.random.split(splits[8], N_REP)).reshape((N_REP, PAGES)).astype(jnp.int32)
    routes_keys = jax.random.split(jax.random.fold_in(splits[9], 1), TOKENS // TOK_DEV)
    routes_turns = jax.random.permutation(jax.random.fold_in(splits[9], 3), TOKENS // TOK_DEV)
    routes = jax.vmap(lambda own, number: routed_block(jax.random.fold_in(splits[9], 2), own, number, TOK_DEV, E, TOP, CAP, 2))(routes_keys, routes_turns).reshape((TOKENS, TOP))
    gates = jnp.clip(jnp.exp(math.log(1.0) - 1.6133518 * jax.random.uniform(splits[10], (TOKENS, TOP), jnp.float32) ** level_of(splits[10], (TOKENS, TOP), ((0, 32),), -0.2, 0.2)), 0.19921875, 1.0).astype(jnp.bfloat16)
    return {"tokens": tokens, "attn_in": attn_in, "attn_out": attn_out, "expert_in": expert_in, "expert_out": expert_out, "attn_gain": attn_gain, "moe_gain": moe_gain, "lengths": lengths, "page_table": page_table, "routes": routes, "gates": gates}


def rms_scale(values, gain):
    values = values.astype(jnp.float32)
    mean_sq = lax.optimization_barrier(jnp.mean(values * values, axis=-1, keepdims=True))
    return values * lax.rsqrt(mean_sq + 1e-06) * gain

def rotate(values, position):
    half = values.shape[-1] // 2
    steps_all = jnp.arange(half, dtype=jnp.float32)
    frequency = jnp.exp(steps_all * (-2.0 * math.log(10000.0) / values.shape[-1]))
    angle = position[:, None] * frequency[None, :]
    cosine = jnp.cos(angle)[:, None, :]
    sine = jnp.sin(angle)[:, None, :]
    front = values[..., :half]
    behind = values[..., half:]
    return jnp.concatenate([front * cosine - behind * sine, behind * cosine + front * sine], axis=-1)

def segment_info(lengths, count):
    lengths = lengths.astype(jnp.int32)
    starts = (jnp.cumsum(lengths) - lengths).astype(jnp.int32)
    index = jnp.arange(count, dtype=jnp.int32)
    member = (index[:, None] >= starts[None, :]).astype(jnp.int32)
    segment = (lax.optimization_barrier(jnp.sum(member, axis=1)) - 1).astype(jnp.int32)
    owner = segment[:, None] == jnp.arange(lengths.shape[0], dtype=jnp.int32)[None, :]
    begin = lax.optimization_barrier(jnp.sum(jnp.where(owner, starts[None, :], 0), axis=1)).astype(jnp.int32)
    return (segment, (index - begin).astype(jnp.int32))

def one_group(tokens, lengths, table, routes, gates, w_qkv, w_mix, w_in, w_out, attn_gain, moe_gain):
    count = tokens.shape[0]
    heads_per = QH // KVH
    segment, position = segment_info(lengths, count)
    index = jnp.arange(count, dtype=jnp.int32)
    normed = rms_scale(tokens, attn_gain).astype(jnp.bfloat16)
    projected = jnp.dot(normed, w_qkv, preferred_element_type=jnp.float32)
    angle_pos = position.astype(jnp.float32)
    queries = rotate(projected[:, :QW].reshape(count, QH, HD), angle_pos).astype(jnp.bfloat16)
    keys = rotate(projected[:, QW:QW + KVH * HD].reshape(count, KVH, HD), angle_pos).astype(jnp.bfloat16)
    values = projected[:, QW + KVH * HD:].astype(jnp.bfloat16)
    grouped = queries.reshape(count, KVH, heads_per, HD).astype(jnp.float32)
    scores = jnp.einsum('igrd,jgd->grij', grouped, keys.astype(jnp.float32)) / math.sqrt(HD)
    allowed = (segment[:, None] == segment[None, :]) & (index[None, :] <= index[:, None])
    scores = jnp.where(allowed[None, None], scores, jnp.float32(-1e+30))
    highest = lax.optimization_barrier(jnp.max(scores, axis=-1, keepdims=True))
    weights = jnp.exp(scores - highest)
    probs = (weights / lax.optimization_barrier(jnp.sum(weights, axis=-1, keepdims=True))).astype(jnp.bfloat16)
    value_heads = values.reshape(count, KVH, HD).astype(jnp.float32)
    attended = jnp.einsum('grij,jgd->igrd', probs.astype(jnp.float32), value_heads)
    attended = attended.astype(jnp.bfloat16).reshape(count, QW)
    hidden = tokens.astype(jnp.float32) + jnp.dot(attended, w_mix, preferred_element_type=jnp.float32)
    normed_two = rms_scale(hidden, moe_gain).astype(jnp.bfloat16)
    depth = N_BLK * CAP

    def add_expert(total, expert):
        hits = routes == expert
        routed = jnp.any(hits, axis=1)
        weight = lax.optimization_barrier(jnp.sum(jnp.where(hits, gates.astype(jnp.float32), jnp.float32(0.0)), axis=1))
        order = jnp.argsort(jnp.where(routed, index, index + count))[:depth].astype(jnp.int32)
        chosen = normed_two[order]
        gate_up = jnp.dot(chosen, w_in[expert], preferred_element_type=jnp.float32)
        activated = (jax.nn.relu(gate_up[:, :FF]) * gate_up[:, FF:]).astype(jnp.bfloat16)
        result = jnp.dot(activated, w_out[expert], preferred_element_type=jnp.float32).astype(jnp.bfloat16)
        return (total.at[order].add(weight[order][:, None] * result.astype(jnp.float32)), None)
    expert_term, _ = lax.scan(add_expert, jnp.zeros((count, D), jnp.float32), jnp.arange(E, dtype=jnp.int32))
    mixed = (hidden + expert_term).astype(jnp.bfloat16)
    cache = jnp.concatenate([keys.reshape(count, KVH * HD), values], axis=1).reshape(count // PAGE, PAGE, KVW)
    pages = jnp.zeros_like(cache).at[table.astype(jnp.int32)].set(cache)
    return (mixed, pages)

def reference(tokens, attn_in, attn_out, expert_in, expert_out, attn_gain, moe_gain, lengths, page_table, routes, gates):
    w_qkv = attn_in.astype(jnp.bfloat16)
    w_mix = attn_out.astype(jnp.bfloat16)
    w_in = expert_in.astype(jnp.bfloat16)
    w_out = expert_out.astype(jnp.bfloat16)

    def run(item):
        group_tokens, group_lengths, group_table, group_routes, group_gates = item
        return one_group(group_tokens, group_lengths, group_table, group_routes, group_gates, w_qkv, w_mix, w_in, w_out, attn_gain, moe_gain)
    mixed, pages = lax.map(run, (tokens.reshape(N_REP, GROUP, D), lengths, page_table, routes.reshape(N_REP, GROUP, TOP), gates.reshape(N_REP, GROUP, TOP)))
    return (mixed.reshape(TOKENS, D), pages.reshape(N_REP * PAGES, PAGE, KVW))
```

```python
import functools
import math

import jax
import jax.numpy as jnp
from jax import lax
from jax.experimental import pallas as pl
from jax.experimental.pallas import tpu as pltpu
from jax.sharding import PartitionSpec as P

D = 1536
FF = 768
QH = 12
KVH = 2
HD = 128
E = 16
PAGE = 128
QW = 1536
QKV = 2048
HALF = QKV // 2
COLS = 256
CHUNKS = 4
BF = jnp.bfloat16
F32 = jnp.float32
VMEM = 56 * 1024 * 1024


def rms_scale(values, gain):
    values = values.astype(F32)
    mean_sq = jnp.mean(values * values, axis=-1, keepdims=True)
    return values * lax.rsqrt(mean_sq + 1e-06) * gain


def rotation(position):
    half = HD // 2
    steps_all = jnp.arange(half, dtype=F32)
    frequency = jnp.exp(steps_all * (-2.0 * math.log(10000.0) / HD))
    angle = position[:, None] * frequency[None, :]
    cosine = jnp.cos(angle)
    sine = jnp.sin(angle)
    return (
        jnp.concatenate([cosine, cosine], axis=1),
        jnp.concatenate([-sine, sine], axis=1),
    )


def segment_begin(lengths, index):
    starts = jnp.cumsum(lengths) - lengths
    member = index[:, None] >= starts[None, :]
    return jnp.max(jnp.where(member, starts[None, :], 0), axis=1)


def project_kernel(pieces, rows, *refs):
    x_ref, cos_ref, sin_ref = refs[:3]
    weights = refs[3 : 3 + 2 * pieces]
    out_ref, held = refs[3 + 2 * pieces :]
    step = pl.program_id(0)

    @pl.when(step < HALF // COLS)
    def _():
        for p in range(pieces):
            held[p * rows : (p + 1) * rows, :] = weights[p][...]

    @pl.when(step >= HALF // COLS)
    def _():
        for p in range(pieces):
            held[p * rows : (p + 1) * rows, :] = weights[pieces + p][...]

    result = jnp.dot(x_ref[...], held[...], preferred_element_type=F32)

    @pl.when(step < (QW + KVH * HD) // COLS)
    def _():
        for h in range(COLS // HD):
            value = result[:, h * HD : (h + 1) * HD]
            turned = value * cos_ref[...] + pltpu.roll(value, HD // 2, 1) * sin_ref[...]
            out_ref[:, h * HD : (h + 1) * HD] = turned.astype(BF)

    @pl.when(step >= (QW + KVH * HD) // COLS)
    def _():
        out_ref[...] = result.astype(BF)


def project(x, cosine, sine, first, second):
    count = x.shape[0]
    pieces, rows = len(first), first[0].shape[0]
    steps = HALF // COLS
    whole = lambda j: (0, 0)
    return pl.pallas_call(
        functools.partial(project_kernel, pieces, rows),
        grid=(2 * steps,),
        in_specs=[
            pl.BlockSpec((count, D), whole),
            pl.BlockSpec((count, HD), whole),
            pl.BlockSpec((count, HD), whole),
        ]
        + [pl.BlockSpec((rows, COLS), lambda j: (0, jnp.minimum(j, steps - 1)))] * pieces
        + [pl.BlockSpec((rows, COLS), lambda j: (0, jnp.maximum(j - steps, 0)))] * pieces,
        out_specs=pl.BlockSpec((count, COLS), lambda j: (0, j)),
        out_shape=jax.ShapeDtypeStruct((count, QKV), BF),
        scratch_shapes=[pltpu.VMEM((D, COLS), BF)],
        compiler_params=pltpu.CompilerParams(vmem_limit_bytes=VMEM),
        cost_estimate=pl.CostEstimate(
            flops=2 * count * D * QKV, bytes_accessed=2 * D * QKV + 4 * count * D, transcendentals=0
        ),
        name="project",
    )(x, cosine, sine, *first, *second)


def attend_kernel(q_ref, k_ref, v_ref, begin_ref, index_ref, across_ref, out_ref):
    scores = lax.dot_general(
        q_ref[...], k_ref[...], (((1,), (1,)), ((), ())), preferred_element_type=F32
    ) * (1.0 / math.sqrt(HD))
    across = across_ref[...]
    allowed = (across >= begin_ref[...]) & (across <= index_ref[...])
    scores = jnp.where(allowed, scores, -1e30)
    highest = jnp.max(scores, axis=1, keepdims=True)
    weights = jnp.exp(scores - highest)
    total = jnp.sum(weights, axis=1, keepdims=True)
    probs = (weights / total).astype(BF)
    out_ref[...] = jnp.dot(probs, v_ref[...], preferred_element_type=F32).astype(BF)


def attend(qkv, begin, index):
    count = qkv.shape[0]
    per = QH // KVH
    column = pl.BlockSpec((count, 1), lambda h: (0, 0))
    return pl.pallas_call(
        attend_kernel,
        grid=(QH,),
        in_specs=[
            pl.BlockSpec((count, HD), lambda h: (0, h)),
            pl.BlockSpec((count, HD), lambda h: (0, QH + h // per)),
            pl.BlockSpec((count, HD), lambda h: (0, QH + KVH + h // per)),
            column,
            column,
            pl.BlockSpec((1, count), lambda h: (0, 0)),
        ],
        out_specs=pl.BlockSpec((count, HD), lambda h: (0, h)),
        out_shape=jax.ShapeDtypeStruct((count, QW), BF),
        compiler_params=pltpu.CompilerParams(vmem_limit_bytes=VMEM),
        cost_estimate=pl.CostEstimate(
            flops=4 * QH * count * count * HD,
            bytes_accessed=2 * count * (QKV + QW),
            transcendentals=QH * count * count,
        ),
        name="attend",
    )(qkv, qkv, qkv, begin[:, None], index[:, None], index[None, :])


def mix_kernel(pieces, rows, *refs):
    x_ref, tokens_ref = refs[:2]
    weights = refs[2 : 2 + pieces]
    out_ref, held = refs[2 + pieces :]
    for p in range(pieces):
        held[p * rows : (p + 1) * rows, :] = weights[p][...]
    out_ref[...] = tokens_ref[...].astype(F32) + jnp.dot(
        x_ref[...], held[...], preferred_element_type=F32
    )


def mix(x, tokens, weights):
    count = x.shape[0]
    pieces, rows = len(weights), weights[0].shape[0]
    return pl.pallas_call(
        functools.partial(mix_kernel, pieces, rows),
        grid=(D // COLS,),
        in_specs=[
            pl.BlockSpec((count, QW), lambda j: (0, 0)),
            pl.BlockSpec((count, COLS), lambda j: (0, j)),
        ]
        + [pl.BlockSpec((rows, COLS), lambda j: (0, j))] * pieces,
        out_specs=pl.BlockSpec((count, COLS), lambda j: (0, j)),
        out_shape=jax.ShapeDtypeStruct((count, D), F32),
        scratch_shapes=[pltpu.VMEM((QW, COLS), BF)],
        compiler_params=pltpu.CompilerParams(vmem_limit_bytes=VMEM),
        cost_estimate=pl.CostEstimate(
            flops=2 * count * D * QW, bytes_accessed=2 * D * QW + 8 * count * D, transcendentals=0
        ),
        name="mix",
    )(x, tokens, *weights)


def gate_up_kernel(pieces, rows, width, *refs):
    x_ref, gate_ref = refs[:2]
    weights = refs[2 : 2 + pieces]
    out_ref, held = refs[2 + pieces :]
    for p in range(pieces):
        held[p * rows : (p + 1) * rows, :] = weights[p][0]
    result = jnp.dot(x_ref[...], held[...], preferred_element_type=F32)
    activated = jnp.maximum(result[:, :width], 0.0) * result[:, width:]
    out_ref[0] = (activated * gate_ref[0]).astype(BF)


def gate_up(x, gate, weights):
    count = x.shape[0]
    pieces = len(weights)
    experts, rows, wide = weights[0].shape
    return pl.pallas_call(
        functools.partial(gate_up_kernel, pieces, rows, wide // 2),
        grid=(experts,),
        in_specs=[
            pl.BlockSpec((count, D), lambda e: (0, 0)),
            pl.BlockSpec((1, count, 1), lambda e: (e, 0, 0)),
        ]
        + [pl.BlockSpec((1, rows, wide), lambda e: (e, 0, 0))] * pieces,
        out_specs=pl.BlockSpec((1, count, wide // 2), lambda e: (e, 0, 0)),
        out_shape=jax.ShapeDtypeStruct((experts, count, wide // 2), BF),
        scratch_shapes=[pltpu.VMEM((D, wide), BF)],
        compiler_params=pltpu.CompilerParams(vmem_limit_bytes=VMEM),
        cost_estimate=pl.CostEstimate(
            flops=2 * experts * count * D * wide,
            bytes_accessed=2 * D * (experts * wide + count),
            transcendentals=0,
        ),
        name="gate_up",
    )(x, gate, *weights)


def along_blk(value, step):
    size = lax.axis_size("blk")
    return lax.ppermute(value, "blk", [(i, (i + step) % size) for i in range(size)])


def across_rep(value, mask):
    return lax.ppermute(value, "rep", [(i, i ^ mask) for i in range(lax.axis_size("rep"))])


def chip_gather(value, turn):
    bits = (lax.axis_size("rep") // 2).bit_length() - 1
    held = {0: value}
    for bit in [(i + turn) % bits for i in range(bits)]:
        held.update({k ^ (1 << bit): across_rep(v, 2 << bit) for k, v in sorted(held.items())})
    return [held[k] for k in sorted(held)]


def order_matrix(chip, core, place, rows, order):
    chips, cycle_size = lax.axis_size("rep") // 2, lax.axis_size("blk")
    sizes = {"chip": chips, "core": 2, "turn": cycle_size}
    spot = jnp.arange(D, dtype=jnp.int32)
    inner, rest, part = spot % rows, spot // rows, {}
    for name in reversed(order):
        part[name], rest = rest % sizes[name], rest // sizes[name]
    rep = (chip ^ part["chip"]) * 2 + (core ^ part["core"])
    blk = (place - part["turn"] + cycle_size) % cycle_size
    source = (rep * cycle_size + blk) * rows + inner
    return (spot[:, None] == source[None, :]).astype(BF)


def body(
    tokens,
    attn_in,
    attn_out,
    expert_in,
    expert_out,
    attn_gain,
    moe_gain,
    lengths,
    page_table,
    routes,
    gates,
):
    count = tokens.shape[0]
    reps, cycle_size = lax.axis_size("rep"), lax.axis_size("blk")
    rep, place = lax.axis_index("rep"), lax.axis_index("blk")
    chip, core = rep // 2, rep % 2
    group_rows = count * cycle_size
    shifts = range(1, cycle_size)
    half_experts = E // 2
    quarter = FF // cycle_size
    rows_in, rows_out = expert_in.shape[1], expert_out.shape[1]

    expert_ids = jnp.arange(E, dtype=jnp.int32)
    dense = jnp.sum(
        jnp.where(
            routes[:, :, None] == expert_ids[None, None, :],
            gates.astype(F32)[:, :, None],
            F32(0.0),
        ),
        axis=1,
    ).astype(BF)

    qkv_here, mix_here = attn_in.astype(BF), attn_out.astype(BF)
    qkv_line = jnp.concatenate([qkv_here] + [along_blk(qkv_here, s) for s in shifts], axis=0)
    mix_line = jnp.concatenate([mix_here] + [along_blk(mix_here, s) for s in shifts], axis=0)
    first_own = chip_gather(qkv_line[:, :HALF], 0)
    second_own = chip_gather(qkv_line[:, HALF:], 1)
    mix_own = chip_gather(mix_line, 1)
    first = first_own + [across_rep(v, 1) for v in first_own]
    second = second_own + [across_rep(v, 1) for v in second_own]
    mixing = mix_own + [across_rep(v, 1) for v in mix_own]

    sent = jnp.concatenate([tokens, jnp.pad(dense, ((0, 0), (0, 128 - E)))], axis=1)
    line = jnp.concatenate([sent] + [along_blk(sent, s) for s in shifts], axis=0)
    group, group_gates = line[:, :D], line[:, D : D + E]

    def split_cores(value):
        mine = lax.dynamic_slice_in_dim(value, core * half_experts, half_experts, 0)
        other = lax.dynamic_slice_in_dim(value, (1 - core) * half_experts, half_experts, 0)
        return jnp.stack([mine, across_rep(other, 1)], axis=1)

    down = split_cores(expert_out.astype(BF)).reshape(half_experts, 2 * rows_out, D)
    down_parts = [
        chip_gather(down[: half_experts // 2], 0),
        chip_gather(down[half_experts // 2 :], 1),
    ]
    down_all = jnp.concatenate(
        [
            jnp.stack([p.reshape(p.shape[0], 2, rows_out, D) for p in part], axis=1).reshape(
                -1, reps, rows_out, D
            )
            for part in down_parts
        ],
        axis=0,
    )
    down_all = jnp.take(down_all, jnp.arange(reps, dtype=jnp.int32) ^ rep, axis=1)
    down_all = down_all.reshape(half_experts * quarter, D)

    spot = jnp.arange(2 * FF, dtype=jnp.int32)
    inner = spot % rows_out
    from_rep = (spot // rows_out) % reps
    which = (spot // quarter) % 2
    from_blk = spot // (2 * quarter)
    column = which * FF + (from_rep * cycle_size + from_blk) * rows_out + inner
    shuffle = (spot[:, None] == column[None, :]).astype(BF)
    ordered = jnp.dot(
        expert_in.astype(BF).reshape(E * rows_in, 2 * FF), shuffle, preferred_element_type=F32
    )
    pairs = split_cores(ordered.astype(BF).reshape(E, rows_in, 2 * FF))
    per_chunk = half_experts // CHUNKS
    up_parts = []
    for n in range(CHUNKS):
        chunk = pairs[n * per_chunk : (n + 1) * per_chunk]
        cut = lambda s: lax.dynamic_slice_in_dim(
            chunk, ((place + s) % cycle_size) * 2 * quarter, 2 * quarter, 3
        )
        pieces = [cut(0)] + [along_blk(cut(s), s) for s in shifts]
        lined = jnp.stack(pieces, axis=1).reshape(per_chunk, cycle_size * 2 * rows_in, 2 * quarter)
        up_parts.append(chip_gather(lined, n))

    index = (
        ((place - jnp.arange(cycle_size, dtype=jnp.int32) + cycle_size) % cycle_size)[:, None] * count
        + jnp.arange(count, dtype=jnp.int32)[None, :]
    ).reshape(group_rows)
    begin = segment_begin(lengths[0], index)
    cosine, sine = rotation((index - begin).astype(F32))
    normed = rms_scale(group, attn_gain).astype(BF)
    order = order_matrix(chip, core, place, rows_in, ("core", "chip", "turn"))
    normed = jnp.dot(normed, order, preferred_element_type=F32).astype(BF)
    qkv = project(normed, cosine, sine, first, second)
    attended = attend(qkv, begin, index)
    attended = jnp.dot(attended, order, preferred_element_type=F32).astype(BF)
    hidden = mix(attended, group, mixing)

    page_count = count // PAGE
    targets = place * page_count + jnp.arange(page_count, dtype=jnp.int32)
    table = page_table[0]
    logical = jnp.sum(
        jnp.where(
            table[None, :] == targets[:, None],
            jnp.arange(table.shape[0], dtype=jnp.int32)[None, :],
            0,
        ),
        axis=1,
    )
    turned = (place - logical // page_count + cycle_size) % cycle_size
    first_row = turned * count + (logical % page_count) * PAGE
    cache = qkv[:, QW:]
    kv_pages = jnp.stack(
        [lax.dynamic_slice_in_dim(cache, first_row[i], PAGE, 0) for i in range(page_count)]
    )

    normed_two = rms_scale(hidden, moe_gain).astype(BF)
    both = jnp.concatenate([normed_two, across_rep(normed_two, 1)], axis=0)
    both_gates = jnp.concatenate([group_gates, across_rep(group_gates, 1)], axis=0)
    my_gates = lax.dynamic_slice_in_dim(both_gates, core * half_experts, half_experts, 1)
    my_gates = my_gates.astype(F32).T[:, :, None]
    order_two = order_matrix(chip, core, place, rows_in, ("chip", "turn", "core"))
    both = jnp.dot(both, order_two, preferred_element_type=F32).astype(BF)
    activated = jnp.concatenate(
        [
            gate_up(both, my_gates[n * per_chunk : (n + 1) * per_chunk], up_parts[n])
            for n in range(CHUNKS)
        ],
        axis=0,
    )
    activated = activated.transpose(1, 0, 2).reshape(2 * group_rows, half_experts * quarter)
    other = jnp.dot(activated[group_rows:], down_all, preferred_element_type=F32).astype(BF)
    mine = jnp.dot(activated[:group_rows], down_all, preferred_element_type=F32)
    summed = mine + across_rep(other, 1).astype(F32)
    total = hidden[:count] + summed[:count]
    for s in shifts:
        part = summed[s * count : (s + 1) * count].astype(BF)
        total = total + along_blk(part, -s).astype(F32)
    return (total.astype(BF), kv_pages)


def solution(mesh):
    in_specs = (
        P(("rep", "blk"), None),
        P(("rep", "blk"), None),
        P(("rep", "blk"), None),
        P(None, ("rep", "blk"), None),
        P(None, ("rep", "blk"), None),
        P(),
        P(),
        P("rep", None),
        P("rep", None),
        P(("rep", "blk"), None),
        P(("rep", "blk"), None),
    )
    out_specs = (P(("rep", "blk"), None), P(("rep", "blk"), None, None))
    return jax.shard_map(body, mesh=mesh, in_specs=in_specs, out_specs=out_specs, check_vma=False)
```

```python
import functools
import math

import jax
import jax.numpy as jnp
from jax import lax
from jax.experimental import pallas as pl
from jax.experimental.pallas import tpu as pltpu
from jax.sharding import PartitionSpec as P

D = 1536
FF = 768
QH = 12
KVH = 2
HD = 128
E = 16
PAGE = 128
QW = 1536
QKV = 2048
WIDE = 512
ROWS = 256
PARTS = 2
CHUNKS = 2
BF = jnp.bfloat16
F32 = jnp.float32
VMEM = 56 * 1024 * 1024


def rms_scale(values, gain):
    values = values.astype(F32)
    mean_sq = jnp.mean(values * values, axis=-1, keepdims=True)
    return values * lax.rsqrt(mean_sq + 1e-06) * gain


def rotation(position):
    half = HD // 2
    steps_all = jnp.arange(half, dtype=F32)
    frequency = jnp.exp(steps_all * (-2.0 * math.log(10000.0) / HD))
    angle = position[:, None] * frequency[None, :]
    cosine = jnp.cos(angle)
    sine = jnp.sin(angle)
    return (
        jnp.concatenate([cosine, cosine], axis=1),
        jnp.concatenate([-sine, sine], axis=1),
    )


def segment_begin(lengths, index):
    starts = jnp.cumsum(lengths) - lengths
    member = index[:, None] >= starts[None, :]
    return jnp.max(jnp.where(member, starts[None, :], 0), axis=1)


def put(held, spots, first, block, value):
    rows = value.shape[0]
    if block % 16 != 0:
        held[pl.ds(first * block, rows), :] = value[...]
        return
    for k in range(rows // block):
        spot = pl.multiple_of(spots[first + k], block)
        held[pl.ds(spot, block), :] = value[k * block : (k + 1) * block, :]


def put_all(held, spots, block, pieces):
    first = 0
    for ref in pieces:
        for n in range(ref.shape[0]):
            put(held, spots, first, block, ref.at[n])
            first += ref.shape[1] // block


def project_kernel(pieces, block, spots, *refs):
    x_ref, cos_ref, sin_ref = refs[:3]
    out_ref, held = refs[3 + pieces :]
    step = pl.program_id(0)
    put_all(held, spots, block, refs[3 : 3 + pieces])
    result = jnp.dot(x_ref[...], held[...], preferred_element_type=F32)
    turning = (QW + KVH * HD) // HD
    for h in range(WIDE // HD):
        value = result[:, h * HD : (h + 1) * HD]
        turned = value * cos_ref[...] + pltpu.roll(value, HD // 2, 1) * sin_ref[...]
        value = jnp.where(step * (WIDE // HD) + h < turning, turned, value)
        out_ref[:, h * HD : (h + 1) * HD] = value.astype(BF)


def project(spots, block, x, cosine, sine, weights):
    count = x.shape[0]
    whole = lambda j, _: (0, 0)
    return pl.pallas_call(
        functools.partial(project_kernel, len(weights), block),
        grid_spec=pltpu.PrefetchScalarGridSpec(
            num_scalar_prefetch=1,
            grid=(QKV // WIDE,),
            in_specs=[
                pl.BlockSpec((count, D), whole),
                pl.BlockSpec((count, HD), whole),
                pl.BlockSpec((count, HD), whole),
            ]
            + [pl.BlockSpec(w.shape[:2] + (WIDE,), lambda j, _: (0, 0, j)) for w in weights],
            out_specs=pl.BlockSpec((count, WIDE), lambda j, _: (0, j)),
            scratch_shapes=[pltpu.VMEM((D, WIDE), BF)],
        ),
        out_shape=jax.ShapeDtypeStruct((count, QKV), BF),
        compiler_params=pltpu.CompilerParams(vmem_limit_bytes=VMEM),
        cost_estimate=pl.CostEstimate(
            flops=2 * count * D * QKV, bytes_accessed=2 * D * QKV + 4 * count * D, transcendentals=0
        ),
        name="project",
    )(spots, x, cosine, sine, *weights)


def attend_kernel(q_ref, k_ref, v_ref, begin_ref, across_ref, out_ref):
    count = q_ref.shape[0]
    for first in range(0, count, ROWS):
        rows, seen = slice(first, first + ROWS), first + ROWS
        scores = lax.dot_general(
            q_ref[rows, :], k_ref[:seen, :], (((1,), (1,)), ((), ())), preferred_element_type=F32
        ) * (1.0 / math.sqrt(HD))
        across = across_ref[:, :seen]
        mine = first + lax.broadcasted_iota(jnp.int32, (ROWS, 1), 0)
        allowed = (across >= begin_ref[rows, :]) & (across <= mine)
        scores = jnp.where(allowed, scores, -1e30)
        highest = jnp.max(scores, axis=1, keepdims=True)
        weights = jnp.exp(scores - highest)
        total = jnp.sum(weights, axis=1, keepdims=True)
        mixed = jnp.dot(weights.astype(BF), v_ref[:seen, :], preferred_element_type=F32)
        out_ref[rows, :] = (mixed / total).astype(BF)


def attend(qkv, begin, index):
    count = qkv.shape[0]
    per = QH // KVH
    column = pl.BlockSpec((count, 1), lambda h: (0, 0))
    return pl.pallas_call(
        attend_kernel,
        grid=(QH,),
        in_specs=[
            pl.BlockSpec((count, HD), lambda h: (0, h)),
            pl.BlockSpec((count, HD), lambda h: (0, QH + h // per)),
            pl.BlockSpec((count, HD), lambda h: (0, QH + KVH + h // per)),
            column,
            pl.BlockSpec((1, count), lambda h: (0, 0)),
        ],
        out_specs=pl.BlockSpec((count, HD), lambda h: (0, h)),
        out_shape=jax.ShapeDtypeStruct((count, QW), BF),
        compiler_params=pltpu.CompilerParams(vmem_limit_bytes=VMEM),
        cost_estimate=pl.CostEstimate(
            flops=4 * QH * count * count * HD,
            bytes_accessed=2 * count * (QKV + QW),
            transcendentals=QH * count * count,
        ),
        name="attend",
    )(qkv, qkv, qkv, begin[:, None], index[None, :])


def mix_kernel(pieces, block, spots, *refs):
    x_ref, tokens_ref = refs[:2]
    out_ref, held = refs[2 + pieces :]
    put_all(held, spots, block, refs[2 : 2 + pieces])
    out_ref[...] = tokens_ref[...].astype(F32) + jnp.dot(
        x_ref[...], held[...], preferred_element_type=F32
    )


def mix(spots, block, x, tokens, weights):
    count = x.shape[0]
    return pl.pallas_call(
        functools.partial(mix_kernel, len(weights), block),
        grid_spec=pltpu.PrefetchScalarGridSpec(
            num_scalar_prefetch=1,
            grid=(D // WIDE,),
            in_specs=[
                pl.BlockSpec((count, QW), lambda j, _: (0, 0)),
                pl.BlockSpec((count, WIDE), lambda j, _: (0, j)),
            ]
            + [pl.BlockSpec(w.shape[:2] + (WIDE,), lambda j, _: (0, 0, j)) for w in weights],
            out_specs=pl.BlockSpec((count, WIDE), lambda j, _: (0, j)),
            scratch_shapes=[pltpu.VMEM((QW, WIDE), BF)],
        ),
        out_shape=jax.ShapeDtypeStruct((count, D), F32),
        compiler_params=pltpu.CompilerParams(vmem_limit_bytes=VMEM),
        cost_estimate=pl.CostEstimate(
            flops=2 * count * D * QW, bytes_accessed=2 * D * QW + 8 * count * D, transcendentals=0
        ),
        name="mix",
    )(spots, x, tokens, *weights)


def norm_kernel(span, spots, x_ref, gain_ref, out_ref, held):
    value = x_ref[...]
    mean_sq = jnp.mean(value * value, axis=1, keepdims=True)
    held[...] = (value * lax.rsqrt(mean_sq + 1e-06) * gain_ref[...]).astype(BF)
    for k in range(D // span):
        spot = pl.multiple_of(spots[k], span) if span % 128 == 0 else k * span
        out_ref[:, k * span : (k + 1) * span] = held[:, pl.ds(spot, span)]


def norm_blocks(spots, span, x, gain):
    count = x.shape[0]
    out = pl.pallas_call(
        functools.partial(norm_kernel, span),
        grid_spec=pltpu.PrefetchScalarGridSpec(
            num_scalar_prefetch=1,
            grid=(count // 128,),
            in_specs=[
                pl.BlockSpec((128, D), lambda i, _: (i, 0)),
                pl.BlockSpec((1, D), lambda i, _: (0, 0)),
            ],
            out_specs=pl.BlockSpec((128, D), lambda i, _: (i, 0)),
            scratch_shapes=[pltpu.VMEM((128, D), BF)],
        ),
        out_shape=jax.ShapeDtypeStruct((count, D), BF),
        compiler_params=pltpu.CompilerParams(vmem_limit_bytes=VMEM),
        cost_estimate=pl.CostEstimate(
            flops=4 * count * D, bytes_accessed=6 * count * D, transcendentals=count
        ),
        name="norm",
    )(spots, x, gain[None, :])
    if span % 128 == 0:
        return out
    return jnp.concatenate(
        [lax.dynamic_slice_in_dim(out, spots[k], span, 1) for k in range(D // span)], axis=1
    )


def gate_up_kernel(orders, mine_ref, other_ref, gate_ref, *refs):
    weights, out_ref = refs[:-1], refs[-1]
    wide = weights[0].shape[1]
    width, span = wide // 4, D // len(orders[0])

    def one(x_ref):
        for p, order in enumerate(orders):
            some = len(order) // 2
            result = None
            for side in range(2):
                blocks = order[side * some : (side + 1) * some]
                if blocks == list(range(blocks[0], blocks[0] + some)):
                    x = x_ref[:, blocks[0] * span : (blocks[0] + some) * span]
                else:
                    x = jnp.concatenate(
                        [x_ref[:, k * span : (k + 1) * span] for k in blocks], axis=1
                    )
                term = jnp.dot(x, weights[2 * p + side][...], preferred_element_type=F32)
                result = term if result is None else result + term
            for e in range(2):
                n = 2 * p + e
                gate = result[:, 2 * e * width : (2 * e + 1) * width]
                up = result[:, (2 * e + 1) * width : (2 * e + 2) * width]
                activated = jnp.maximum(gate, 0.0) * up * gate_ref[:, n : n + 1]
                out_ref[:, n * width : (n + 1) * width] = activated.astype(BF)

    @pl.when(pl.program_id(0) == 0)
    def _():
        one(mine_ref)

    @pl.when(pl.program_id(0) == 1)
    def _():
        one(other_ref)


def gate_up(orders, mine, other, gate, weights):
    count, experts = mine.shape[0], gate.shape[1]
    deep, wide = weights[0].shape
    whole = pl.BlockSpec((deep, wide), lambda i: (0, 0))
    rows = pl.BlockSpec((count, D), lambda i: (0, 0))
    return pl.pallas_call(
        functools.partial(gate_up_kernel, orders),
        grid=(2,),
        in_specs=[rows, rows, pl.BlockSpec((count, experts), lambda i: (i, 0))]
        + [whole] * len(weights),
        out_specs=pl.BlockSpec((count, experts * wide // 4), lambda i: (i, 0)),
        out_shape=jax.ShapeDtypeStruct((2 * count, experts * wide // 4), BF),
        compiler_params=pltpu.CompilerParams(vmem_limit_bytes=VMEM),
        cost_estimate=pl.CostEstimate(
            flops=2 * experts * count * D * wide,
            bytes_accessed=D * (experts * wide + 4 * count),
            transcendentals=0,
        ),
        name="gate_up",
    )(mine, other, gate, *weights)


def down_kernel(parts, block, spots, *refs):
    acts, weights = refs[:parts], refs[parts:-4]
    mine_ref, other_ref, held, side = refs[-4:]
    deep = acts[0].shape[1]
    for n, act in enumerate(acts):
        side[:, n * deep : (n + 1) * deep] = act[...]
    span = held.shape[0] // E * 2
    experts = weights[0].shape[1]
    stacks = 2 if block % 16 == 0 else 1
    for n in range(0, len(weights), stacks):
        for e in range(experts):
            first = (n // stacks * experts + e) * span
            put_all(
                held.at[pl.ds(first, span)],
                spots.at[n // stacks],
                block,
                [w.at[:, e] for w in weights[n : n + stacks]],
            )
    half = side.shape[0] // 2
    total = jnp.dot(side[half:, :], held[...], preferred_element_type=F32)
    other_ref[...] = total.astype(other_ref.dtype)
    mine_ref[...] = jnp.dot(side[:half, :], held[...], preferred_element_type=F32)


def down_project(spots, block, acts, part, parts, weights):
    rows, deep = acts[0].shape
    total, wide = deep * len(acts), D // parts
    return pl.pallas_call(
        functools.partial(down_kernel, len(acts), block),
        grid_spec=pltpu.PrefetchScalarGridSpec(
            num_scalar_prefetch=1,
            grid=(1,),
            in_specs=[pl.BlockSpec((rows, deep), lambda j, _: (0, 0))] * len(acts)
            + [pl.BlockSpec(w.shape[:3] + (wide,), lambda j, _: (0, 0, 0, part)) for w in weights],
            out_specs=[pl.BlockSpec((rows // 2, wide), lambda j, _: (0, 0))] * 2,
            scratch_shapes=[pltpu.VMEM((total, wide), BF), pltpu.VMEM((rows, total), BF)],
        ),
        out_shape=[
            jax.ShapeDtypeStruct((rows // 2, wide), F32),
            jax.ShapeDtypeStruct((rows // 2, wide), BF),
        ],
        compiler_params=pltpu.CompilerParams(vmem_limit_bytes=VMEM),
        cost_estimate=pl.CostEstimate(
            flops=2 * rows * wide * total,
            bytes_accessed=2 * wide * total + 2 * rows * total + 3 * rows * wide,
            transcendentals=0,
        ),
        name="down",
    )(spots, *acts, *weights)


def along_blk(value, step):
    size = lax.axis_size("blk")
    return lax.ppermute(value, "blk", [(i, (i + step) % size) for i in range(size)])


def across_rep(value, mask):
    return lax.ppermute(value, "rep", [(i, i ^ mask) for i in range(lax.axis_size("rep"))])


def chip_bits():
    return (lax.axis_size("rep") // 2).bit_length() - 1


def chip_bits():
    return (lax.axis_size("rep") // 2).bit_length() - 1


def chip_start(value, turn):
    return value[None], across_rep(value[None], 2 << turn)


def chip_gather(held, came, turn, gate=()):
    bits = chip_bits()
    for n in range(1, bits):
        held = jnp.concatenate([held, came], axis=0)
        came = across_rep(after(held, gate), 2 << ((n + turn) % bits))
    return [held, came]


def chip_order(turn):
    bits = chip_bits()
    order = [0]
    for n in range(bits):
        order = order + [k ^ (1 << ((n + turn) % bits)) for k in order]
    return order


def after(value, other):
    if isinstance(other, tuple) and not other:
        return value
    return lax.optimization_barrier((value, other))[0]


def exchange_blk(value):
    return lax.all_to_all(value, "blk", 0, 0, tiled=True)


def gather_blk(value):
    size = lax.axis_size("blk")
    return exchange_blk(jnp.broadcast_to(value[None], (size,) + value.shape))


def body(
    tokens,
    attn_in,
    attn_out,
    expert_in,
    expert_out,
    attn_gain,
    moe_gain,
    lengths,
    page_table,
    routes,
    gates,
):
    count = tokens.shape[0]
    reps, cycle_size = lax.axis_size("rep"), lax.axis_size("blk")
    rep, place = lax.axis_index("rep"), lax.axis_index("blk")
    chip, core = rep // 2, rep % 2
    group_rows = count * cycle_size
    half_experts = E // 2
    quarter = FF // cycle_size
    rows_in, rows_out = expert_in.shape[1], expert_out.shape[1]

    def split_cores(value):
        half = value.shape[0] // 2
        mine = lax.dynamic_slice_in_dim(value, core * half, half, 0)
        other = lax.dynamic_slice_in_dim(value, (1 - core) * half, half, 0)
        came = across_rep(other, 1)
        return jnp.stack(
            [jnp.where(core == 0, mine, came), jnp.where(core == 0, came, mine)], axis=1
        )

    spot = jnp.arange(2 * FF, dtype=jnp.int32)
    inner = spot % rows_out
    from_rep = (spot // rows_out) % reps
    which = (spot // quarter) % 2
    from_blk = spot // (2 * quarter)
    column = which * FF + (from_rep * cycle_size + from_blk) * rows_out + inner
    shuffle = (spot[:, None] == column[None, :]).astype(BF)
    ordered = jnp.dot(
        expert_in.astype(BF).reshape(E * rows_in, 2 * FF), shuffle, preferred_element_type=F32
    )
    ordered = ordered.astype(BF).reshape(E // 2, 2, rows_in, 2 * FF)
    pairs = jnp.stack(
        [
            jnp.concatenate(
                [
                    lax.slice_in_dim(ordered[:, e], b * 2 * quarter, (b + 1) * 2 * quarter, axis=2)
                    for e in range(2)
                ],
                axis=2,
            )
            for b in range(cycle_size)
        ],
        axis=1,
    )
    pairs = split_cores(pairs)
    per_chunk = half_experts // 2 // CHUNKS

    down = split_cores(expert_out.astype(BF)).reshape(half_experts, 2 * rows_out, D)
    down_first = [chip_start(down[n * 4 : (n + 1) * 4], n % 2) for n in range(half_experts // 4)]

    attn_here = jnp.concatenate([attn_in.astype(BF), attn_out.astype(BF)], axis=1)
    attn_line = gather_blk(attn_here).reshape(cycle_size * rows_in, QKV + D)
    ready = after(attn_line, down_first)
    qkv_first = chip_start(ready[:, :QKV], 0)
    mix_first = chip_start(ready[:, QKV:], 1)
    down_parts = [chip_gather(*down_first[n], n % 2) for n in range(len(down_first))]

    gate = (qkv_first, mix_first, down_parts)
    qkv_own = chip_gather(*qkv_first, 0, gate)
    mix_own = chip_gather(*mix_first, 1, gate)
    qkv_weight = qkv_own + [across_rep(v, 1) for v in qkv_own]
    mix_weight = mix_own + [across_rep(v, 1) for v in mix_own]

    def line_up(n, earlier):
        chunk = pairs[n * per_chunk : (n + 1) * per_chunk].transpose(2, 0, 1, 3, 4)
        lined = exchange_blk(after(chunk, earlier)).transpose(1, 2, 0, 3, 4)
        return lined.reshape(per_chunk, 2 * cycle_size * rows_in, 4 * quarter)

    lines = [line_up(0, (attn_line,))]

    expert_ids = jnp.arange(E, dtype=jnp.int32)
    dense = jnp.sum(
        jnp.where(
            routes[:, :, None] == expert_ids[None, None, :],
            gates.astype(F32)[:, :, None],
            F32(0.0),
        ),
        axis=1,
    ).astype(BF)
    sent = jnp.concatenate([tokens, jnp.pad(dense, ((0, 0), (0, 128 - E)))], axis=1)
    line = gather_blk(after(sent, (lines[0],))).reshape(group_rows, -1)
    group, group_gates = line[:, :D], line[:, D : D + E]

    for n in range(1, CHUNKS):
        lines.append(line_up(n, (line, lines[-1])))

    index = jnp.arange(group_rows, dtype=jnp.int32)
    begin = segment_begin(lengths[0], index)
    cosine, sine = rotation((index - begin).astype(F32))
    block = cycle_size * rows_in

    def attn_spots(turn):
        from_chip = chip ^ jnp.array(chip_order(turn), jnp.int32)
        from_rep = from_chip[None, :] * 2 + (core ^ jnp.arange(2, dtype=jnp.int32))[:, None]
        return (from_rep * block).reshape(-1)

    normed = rms_scale(group, attn_gain).astype(BF)
    up_parts, steps, gate = [], [], ()
    for n in range(CHUNKS):
        lined = after(lines[n], gate)
        first = [chip_start(lined[k], k % 2) for k in range(per_chunk)]
        parts = [chip_gather(*first[k], k % 2) for k in range(per_chunk)]
        up_parts.append([p.reshape(-1, 4 * quarter) for part in parts for p in part])
        steps += [first, parts]
        gate = (parts,)
        if n == 0:
            x = after(normed, (first,))
            qkv = project(attn_spots(0), block, x, cosine, sine, qkv_weight)
            attended = attend(qkv, begin, index)
            gate = (qkv,)
    attended = after(attended, (steps[1],))
    hidden = mix(attn_spots(1), block, attended, group, mix_weight)

    page_count = count // PAGE
    targets = place * page_count + jnp.arange(page_count, dtype=jnp.int32)
    table = page_table[0]
    logical = jnp.sum(
        jnp.where(
            table[None, :] == targets[:, None],
            jnp.arange(table.shape[0], dtype=jnp.int32)[None, :],
            0,
        ),
        axis=1,
    )
    first_row = logical * PAGE
    cache = qkv[:, QW:]
    kv_pages = jnp.stack(
        [lax.dynamic_slice_in_dim(cache, first_row[i], PAGE, 0) for i in range(page_count)]
    )

    span = D // (reps // 2)
    up_spots = (chip ^ jnp.arange(reps // 2, dtype=jnp.int32)) * span
    normed_two = norm_blocks(up_spots, span, hidden, moe_gain)
    other_two = across_rep(normed_two, 1)
    both_gates = jnp.concatenate([group_gates, across_rep(group_gates, 1)], axis=0)
    my_gates = lax.dynamic_slice_in_dim(both_gates, core * half_experts, half_experts, 1).astype(F32)
    acts, orders = [], [chip_order(k % 2) for k in range(per_chunk)]
    for n in range(CHUNKS):
        experts = slice(n * 2 * per_chunk, (n + 1) * 2 * per_chunk)
        x = after(normed_two, (steps[2 * n + 2],)) if n + 1 < CHUNKS else normed_two
        acts.append(gate_up(orders, x, other_two, my_gates[:, experts], up_parts[n]))
    chips, chip_rows = reps // 2, 2 * rows_out
    whose = [chip ^ jnp.array(chip_order(n % 2), jnp.int32) for n in range(len(down_parts))]
    if chip_rows % 16 != 0:
        for n, part in enumerate(down_parts):
            part = jnp.take(jnp.concatenate(part, axis=0), jnp.argsort(whose[n]), axis=0)
            down_parts[n] = [part.transpose(1, 0, 2, 3).reshape(1, 4, chips * chip_rows, D)]
    down = [w for part in down_parts for w in part]
    down_spots = jnp.stack(whose) * chip_rows

    def at(array, shift):
        first = (place + shift) % cycle_size * count
        return lax.dynamic_slice_in_dim(array, first, count, 0).astype(F32)

    mixed, came = [], ()
    for n in range(PARTS):
        ready = after(acts, came)
        mine, other = down_project(down_spots, chip_rows, ready, n, PARTS, down)
        came = across_rep(other, 1)
        columns = slice(n * (D // PARTS), (n + 1) * (D // PARTS))
        total = at(hidden[:, columns], 0) + (at(mine, 0) + at(came, 0))
        for step in range(1, cycle_size):
            part = (at(mine, step) + at(came, step)).astype(BF)
            total = total + along_blk(part, step).astype(F32)
        mixed.append(total.astype(BF))
    return (jnp.concatenate(mixed, axis=1), kv_pages)


def solution(mesh):
    in_specs = (
        P(("rep", "blk"), None),
        P(("rep", "blk"), None),
        P(("rep", "blk"), None),
        P(None, ("rep", "blk"), None),
        P(None, ("rep", "blk"), None),
        P(),
        P(),
        P("rep", None),
        P("rep", None),
        P(("rep", "blk"), None),
        P(("rep", "blk"), None),
    )
    out_specs = (P(("rep", "blk"), None), P(("rep", "blk"), None, None))
    return jax.shard_map(body, mesh=mesh, in_specs=in_specs, out_specs=out_specs, check_vma=False)
```

```python
import functools
import math

import jax
import jax.numpy as jnp
from jax import lax
from jax.experimental import pallas as pl
from jax.experimental.pallas import tpu as pltpu
from jax.sharding import PartitionSpec as P

D = 1536
FF = 768
QH = 12
KVH = 2
HD = 128
E = 16
PAGE = 128
QW = 1536
QKV = 2048
WIDE = 512
ROWS = 256
EASE = 16
CHUNKS = 2
BF = jnp.bfloat16
F32 = jnp.float32
VMEM = 56 * 1024 * 1024


def rms_scale(values, gain):
    values = values.astype(F32)
    mean_sq = jnp.mean(values * values, axis=-1, keepdims=True)
    return values * lax.rsqrt(mean_sq + 1e-06) * gain


def rotation(position):
    half = HD // 2
    steps_all = jnp.arange(half, dtype=F32)
    frequency = jnp.exp(steps_all * (-2.0 * math.log(10000.0) / HD))
    angle = position[:, None] * frequency[None, :]
    cosine = jnp.cos(angle)
    sine = jnp.sin(angle)
    return (
        jnp.concatenate([cosine, cosine], axis=1),
        jnp.concatenate([-sine, sine], axis=1),
    )


def segment_begin(lengths, index):
    starts = jnp.cumsum(lengths) - lengths
    member = index[:, None] >= starts[None, :]
    return jnp.max(jnp.where(member, starts[None, :], 0), axis=1)


def cost(flops, bytes_accessed, transcendentals):
    return pl.CostEstimate(
        flops=flops // EASE, bytes_accessed=bytes_accessed // EASE, transcendentals=transcendentals // EASE
    )


def put(held, spots, first, block, value):
    rows = value.shape[0]
    if block % 16 != 0:
        held[pl.ds(first * block, rows), :] = value[...]
        return
    for k in range(rows // block):
        spot = pl.multiple_of(spots[first + k], block)
        held[pl.ds(spot, block), :] = value[k * block : (k + 1) * block, :]


def put_all(held, spots, block, pieces):
    first = 0
    for ref in pieces:
        for n in range(ref.shape[0]):
            put(held, spots, first, block, ref.at[n])
            first += ref.shape[1] // block


def project_kernel(pieces, block, spots, *refs):
    x_ref, cos_ref, sin_ref = refs[:3]
    out_ref, held = refs[3 + pieces :]
    step = pl.program_id(0)
    put_all(held, spots, block, refs[3 : 3 + pieces])
    result = jnp.dot(x_ref[...], held[...], preferred_element_type=F32)
    turning = (QW + KVH * HD) // HD
    for h in range(WIDE // HD):
        value = result[:, h * HD : (h + 1) * HD]
        turned = value * cos_ref[...] + pltpu.roll(value, HD // 2, 1) * sin_ref[...]
        value = jnp.where(step * (WIDE // HD) + h < turning, turned, value)
        out_ref[:, h * HD : (h + 1) * HD] = value.astype(BF)


def project(spots, block, x, cosine, sine, weights):
    count = x.shape[0]
    whole = lambda j, _: (0, 0)
    return pl.pallas_call(
        functools.partial(project_kernel, len(weights), block),
        grid_spec=pltpu.PrefetchScalarGridSpec(
            num_scalar_prefetch=1,
            grid=(QKV // WIDE,),
            in_specs=[
                pl.BlockSpec((count, D), whole),
                pl.BlockSpec((count, HD), whole),
                pl.BlockSpec((count, HD), whole),
            ]
            + [pl.BlockSpec(w.shape[:2] + (WIDE,), lambda j, _: (0, 0, j)) for w in weights],
            out_specs=pl.BlockSpec((count, WIDE), lambda j, _: (0, j)),
            scratch_shapes=[pltpu.VMEM((D, WIDE), BF)],
        ),
        out_shape=jax.ShapeDtypeStruct((count, QKV), BF),
        compiler_params=pltpu.CompilerParams(vmem_limit_bytes=VMEM),
        cost_estimate=cost(
            flops=2 * count * D * QKV, bytes_accessed=2 * D * QKV + 4 * count * D, transcendentals=0
        ),
        name="project",
    )(spots, x, cosine, sine, *weights)


def attend_kernel(q_ref, k_ref, v_ref, begin_ref, across_ref, out_ref):
    count = q_ref.shape[0]
    for first in range(0, count, ROWS):
        rows, seen = slice(first, first + ROWS), first + ROWS
        scores = lax.dot_general(
            q_ref[rows, :], k_ref[:seen, :], (((1,), (1,)), ((), ())), preferred_element_type=F32
        ) * (1.0 / math.sqrt(HD))
        across = across_ref[:, :seen]
        mine = first + lax.broadcasted_iota(jnp.int32, (ROWS, 1), 0)
        allowed = (across >= begin_ref[rows, :]) & (across <= mine)
        scores = jnp.where(allowed, scores, -1e30)
        highest = jnp.max(scores, axis=1, keepdims=True)
        weights = jnp.exp(scores - highest)
        total = jnp.sum(weights, axis=1, keepdims=True)
        mixed = jnp.dot(weights.astype(BF), v_ref[:seen, :], preferred_element_type=F32)
        out_ref[rows, :] = (mixed / total).astype(BF)


def attend(qkv, begin, index):
    count = qkv.shape[0]
    per = QH // KVH
    column = pl.BlockSpec((count, 1), lambda h: (0, 0))
    return pl.pallas_call(
        attend_kernel,
        grid=(QH,),
        in_specs=[
            pl.BlockSpec((count, HD), lambda h: (0, h)),
            pl.BlockSpec((count, HD), lambda h: (0, QH + h // per)),
            pl.BlockSpec((count, HD), lambda h: (0, QH + KVH + h // per)),
            column,
            pl.BlockSpec((1, count), lambda h: (0, 0)),
        ],
        out_specs=pl.BlockSpec((count, HD), lambda h: (0, h)),
        out_shape=jax.ShapeDtypeStruct((count, QW), BF),
        compiler_params=pltpu.CompilerParams(vmem_limit_bytes=VMEM),
        cost_estimate=cost(
            flops=4 * QH * count * count * HD,
            bytes_accessed=2 * count * (QKV + QW),
            transcendentals=QH * count * count,
        ),
        name="attend",
    )(qkv, qkv, qkv, begin[:, None], index[None, :])


def mix_kernel(pieces, block, spots, *refs):
    x_ref, tokens_ref = refs[:2]
    out_ref, held = refs[2 + pieces :]
    put_all(held, spots, block, refs[2 : 2 + pieces])
    out_ref[...] = tokens_ref[...].astype(F32) + jnp.dot(
        x_ref[...], held[...], preferred_element_type=F32
    )


def mix(spots, block, x, tokens, weights):
    count = x.shape[0]
    return pl.pallas_call(
        functools.partial(mix_kernel, len(weights), block),
        grid_spec=pltpu.PrefetchScalarGridSpec(
            num_scalar_prefetch=1,
            grid=(D // WIDE,),
            in_specs=[
                pl.BlockSpec((count, QW), lambda j, _: (0, 0)),
                pl.BlockSpec((count, WIDE), lambda j, _: (0, j)),
            ]
            + [pl.BlockSpec(w.shape[:2] + (WIDE,), lambda j, _: (0, 0, j)) for w in weights],
            out_specs=pl.BlockSpec((count, WIDE), lambda j, _: (0, j)),
            scratch_shapes=[pltpu.VMEM((QW, WIDE), BF)],
        ),
        out_shape=jax.ShapeDtypeStruct((count, D), F32),
        compiler_params=pltpu.CompilerParams(vmem_limit_bytes=VMEM),
        cost_estimate=cost(
            flops=2 * count * D * QW, bytes_accessed=2 * D * QW + 8 * count * D, transcendentals=0
        ),
        name="mix",
    )(spots, x, tokens, *weights)


def norm_kernel(span, spots, x_ref, gain_ref, out_ref, held):
    value = x_ref[...]
    mean_sq = jnp.mean(value * value, axis=1, keepdims=True)
    held[...] = (value * lax.rsqrt(mean_sq + 1e-06) * gain_ref[...]).astype(BF)
    for k in range(D // span):
        spot = pl.multiple_of(spots[k], span) if span % 128 == 0 else k * span
        out_ref[:, k * span : (k + 1) * span] = held[:, pl.ds(spot, span)]


def norm_blocks(spots, span, x, gain):
    count = x.shape[0]
    out = pl.pallas_call(
        functools.partial(norm_kernel, span),
        grid_spec=pltpu.PrefetchScalarGridSpec(
            num_scalar_prefetch=1,
            grid=(count // 128,),
            in_specs=[
                pl.BlockSpec((128, D), lambda i, _: (i, 0)),
                pl.BlockSpec((1, D), lambda i, _: (0, 0)),
            ],
            out_specs=pl.BlockSpec((128, D), lambda i, _: (i, 0)),
            scratch_shapes=[pltpu.VMEM((128, D), BF)],
        ),
        out_shape=jax.ShapeDtypeStruct((count, D), BF),
        compiler_params=pltpu.CompilerParams(vmem_limit_bytes=VMEM),
        cost_estimate=cost(
            flops=4 * count * D, bytes_accessed=6 * count * D, transcendentals=count
        ),
        name="norm",
    )(spots, x, gain[None, :])
    if span % 128 == 0:
        return out
    return jnp.concatenate(
        [lax.dynamic_slice_in_dim(out, spots[k], span, 1) for k in range(D // span)], axis=1
    )


def gate_up_kernel(orders, mine_ref, other_ref, gate_ref, *refs):
    weights, out_ref = refs[:-1], refs[-1]
    wide = weights[0].shape[1]
    width, span = wide // 4, D // len(orders[0])

    def one(x_ref):
        for p, order in enumerate(orders):
            some = len(order) // 2
            result = None
            for side in range(2):
                blocks = order[side * some : (side + 1) * some]
                if blocks == list(range(blocks[0], blocks[0] + some)):
                    x = x_ref[:, blocks[0] * span : (blocks[0] + some) * span]
                else:
                    x = jnp.concatenate(
                        [x_ref[:, k * span : (k + 1) * span] for k in blocks], axis=1
                    )
                term = jnp.dot(x, weights[2 * p + side][...], preferred_element_type=F32)
                result = term if result is None else result + term
            for e in range(2):
                n = 2 * p + e
                gate = result[:, 2 * e * width : (2 * e + 1) * width]
                up = result[:, (2 * e + 1) * width : (2 * e + 2) * width]
                activated = jnp.maximum(gate, 0.0) * up * gate_ref[:, n : n + 1]
                out_ref[:, n * width : (n + 1) * width] = activated.astype(BF)

    @pl.when(pl.program_id(0) == 0)
    def _():
        one(mine_ref)

    @pl.when(pl.program_id(0) == 1)
    def _():
        one(other_ref)


def gate_up(orders, mine, other, gate, weights):
    count, experts = mine.shape[0], gate.shape[1]
    deep, wide = weights[0].shape
    whole = pl.BlockSpec((deep, wide), lambda i: (0, 0))
    rows = pl.BlockSpec((count, D), lambda i: (0, 0))
    return pl.pallas_call(
        functools.partial(gate_up_kernel, orders),
        grid=(2,),
        in_specs=[rows, rows, pl.BlockSpec((count, experts), lambda i: (i, 0))]
        + [whole] * len(weights),
        out_specs=pl.BlockSpec((count, experts * wide // 4), lambda i: (i, 0)),
        out_shape=jax.ShapeDtypeStruct((2 * count, experts * wide // 4), BF),
        compiler_params=pltpu.CompilerParams(vmem_limit_bytes=VMEM),
        cost_estimate=cost(
            flops=2 * experts * count * D * wide,
            bytes_accessed=D * (experts * wide + 4 * count),
            transcendentals=0,
        ),
        name="gate_up",
    )(mine, other, gate, *weights)


def down_kernel(block, stacks, spots, act_ref, *refs):
    weights, held = refs[:stacks], refs[-1]
    addend, out_ref = refs[stacks:-2], refs[-2]
    experts = weights[0].shape[1]
    span = held.shape[0] // experts
    for e in range(experts):
        put_all(held.at[pl.ds(e * span, span)], spots, block, [w.at[:, e] for w in weights])
    total = jnp.dot(act_ref[...], held[...], preferred_element_type=F32)
    if addend:
        total += addend[0][...]
    out_ref[...] = total.astype(out_ref.dtype)


def down_project(spots, block, act, weights, kind, part=0, parts=1, addend=()):
    rows, deep = act.shape
    rows, wide = rows // parts, D // 2
    return pl.pallas_call(
        functools.partial(down_kernel, block, len(weights)),
        grid_spec=pltpu.PrefetchScalarGridSpec(
            num_scalar_prefetch=1,
            grid=(D // wide,),
            in_specs=[pl.BlockSpec((rows, deep), lambda j, _: (part, 0))]
            + [pl.BlockSpec(w.shape[:3] + (wide,), lambda j, _: (0, 0, 0, j)) for w in weights]
            + [pl.BlockSpec((rows, wide), lambda j, _: (part, j)) for _ in addend],
            out_specs=pl.BlockSpec((rows, wide), lambda j, _: (0, j)),
            scratch_shapes=[pltpu.VMEM((deep, wide), BF)],
        ),
        out_shape=jax.ShapeDtypeStruct((rows, D), kind),
        compiler_params=pltpu.CompilerParams(vmem_limit_bytes=VMEM),
        cost_estimate=cost(
            flops=2 * rows * D * deep,
            bytes_accessed=2 * D * deep + 2 * rows * deep + 8 * rows * D,
            transcendentals=0,
        ),
        name="down",
    )(spots, act, *weights, *addend)


def across_blk(value, mask):
    return lax.ppermute(value, "blk", [(i, i ^ mask) for i in range(lax.axis_size("blk"))])


def across_rep(value, mask):
    return lax.ppermute(value, "rep", [(i, i ^ mask) for i in range(lax.axis_size("rep"))])


def chip_bits():
    return (lax.axis_size("rep") // 2).bit_length() - 1


def chip_bits():
    return (lax.axis_size("rep") // 2).bit_length() - 1


def chip_start(value, turn):
    return value[None], across_rep(value[None], 2 << turn)


def chip_gather(held, came, turn, gate=()):
    bits = chip_bits()
    for n in range(1, bits):
        held = jnp.concatenate([held, came], axis=0)
        came = across_rep(after(held, gate), 2 << ((n + turn) % bits))
    return [held, came]


def chip_order(turn):
    bits = chip_bits()
    order = [0]
    for n in range(bits):
        order = order + [k ^ (1 << ((n + turn) % bits)) for k in order]
    return order


def after(value, other):
    if isinstance(other, tuple) and not other:
        return value
    return lax.optimization_barrier((value, other))[0]


def exchange_blk(value):
    return lax.all_to_all(value, "blk", 0, 0, tiled=True)


def gather_blk(value):
    size = lax.axis_size("blk")
    return exchange_blk(jnp.broadcast_to(value[None], (size,) + value.shape))


def body(
    tokens,
    attn_in,
    attn_out,
    expert_in,
    expert_out,
    attn_gain,
    moe_gain,
    lengths,
    page_table,
    routes,
    gates,
):
    count = tokens.shape[0]
    reps, cycle_size = lax.axis_size("rep"), lax.axis_size("blk")
    rep, place = lax.axis_index("rep"), lax.axis_index("blk")
    chip, core = rep // 2, rep % 2
    group_rows = count * cycle_size
    half_experts = E // 2
    quarter = FF // cycle_size
    rows_in, rows_out = expert_in.shape[1], expert_out.shape[1]

    def split_cores(value):
        half = value.shape[0] // 2
        mine = lax.dynamic_slice_in_dim(value, core * half, half, 0)
        other = lax.dynamic_slice_in_dim(value, (1 - core) * half, half, 0)
        came = across_rep(other, 1)
        return jnp.stack(
            [jnp.where(core == 0, mine, came), jnp.where(core == 0, came, mine)], axis=1
        )

    down = split_cores(expert_out.astype(BF)).reshape(half_experts, 2 * rows_out, D)
    down_first = [chip_start(down[n * 4 : (n + 1) * 4], n % 2) for n in range(half_experts // 4)]

    down_parts = [chip_gather(*down_first[n], n % 2) for n in range(len(down_first))]

    spot = jnp.arange(2 * FF, dtype=jnp.int32)
    inner = spot % rows_out
    from_rep = (spot // rows_out) % reps
    which = (spot // quarter) % 2
    from_blk = spot // (2 * quarter)
    column = which * FF + (from_rep * cycle_size + from_blk) * rows_out + inner
    shuffle = (spot[:, None] == column[None, :]).astype(BF)
    expert_in = after(expert_in, down_first)
    ordered = jnp.dot(
        expert_in.astype(BF).reshape(E * rows_in, 2 * FF), shuffle, preferred_element_type=F32
    )
    ordered = ordered.astype(BF).reshape(E // 2, 2, rows_in, 2 * FF)
    pairs = jnp.stack(
        [
            jnp.concatenate(
                [
                    lax.slice_in_dim(ordered[:, e], b * 2 * quarter, (b + 1) * 2 * quarter, axis=2)
                    for e in range(2)
                ],
                axis=2,
            )
            for b in range(cycle_size)
        ],
        axis=1,
    )
    pairs = split_cores(pairs)
    per_chunk = half_experts // 2 // CHUNKS

    attn_here = jnp.concatenate([attn_in.astype(BF), attn_out.astype(BF)], axis=1)
    attn_line = gather_blk(attn_here).reshape(cycle_size * rows_in, QKV + D)
    ready = after(attn_line, down_parts)
    qkv_first = chip_start(ready[:, :QKV], 0)
    mix_first = chip_start(ready[:, QKV:], 1)

    gate = (qkv_first, mix_first)
    qkv_own = chip_gather(*qkv_first, 0, gate)
    mix_own = chip_gather(*mix_first, 1, gate)
    qkv_weight = qkv_own + [across_rep(v, 1) for v in qkv_own]
    mix_weight = mix_own + [across_rep(v, 1) for v in mix_own]

    def line_up(n, earlier):
        chunk = pairs[n * per_chunk : (n + 1) * per_chunk].transpose(2, 0, 1, 3, 4)
        lined = exchange_blk(after(chunk, earlier)).transpose(1, 2, 0, 3, 4)
        return lined.reshape(per_chunk, 2 * cycle_size * rows_in, 4 * quarter)

    lines = [line_up(0, (attn_line, down_first))]

    expert_ids = jnp.arange(E, dtype=jnp.int32)
    dense = jnp.sum(
        jnp.where(
            routes[:, :, None] == expert_ids[None, None, :],
            gates.astype(F32)[:, :, None],
            F32(0.0),
        ),
        axis=1,
    ).astype(BF)
    sent = jnp.concatenate([tokens, jnp.pad(dense, ((0, 0), (0, 128 - E)))], axis=1)
    line = gather_blk(after(sent, (lines[0], qkv_first, mix_first))).reshape(group_rows, -1)
    group, group_gates = line[:, :D], line[:, D : D + E]

    for n in range(1, CHUNKS):
        lines.append(line_up(n, (line, lines[-1])))

    index = jnp.arange(group_rows, dtype=jnp.int32)
    begin = segment_begin(lengths[0], index)
    cosine, sine = rotation((index - begin).astype(F32))
    block = cycle_size * rows_in

    def attn_spots(turn):
        from_chip = chip ^ jnp.array(chip_order(turn), jnp.int32)
        from_rep = from_chip[None, :] * 2 + (core ^ jnp.arange(2, dtype=jnp.int32))[:, None]
        return (from_rep * block).reshape(-1)

    normed = rms_scale(group, attn_gain).astype(BF)
    up_parts, steps, gate = [], [], ()
    for n in range(CHUNKS):
        lined = after(lines[n], gate)
        first = [chip_start(lined[k], k % 2) for k in range(per_chunk)]
        parts = [chip_gather(*first[k], k % 2) for k in range(per_chunk)]
        up_parts.append([p.reshape(-1, 4 * quarter) for part in parts for p in part])
        steps += [first, parts]
        gate = (parts,)
        if n == 0:
            x = after(normed, (first,))
            qkv = project(attn_spots(0), block, x, cosine, sine, qkv_weight)
            attended = attend(qkv, begin, index)
            gate = (attended,)
    attended = after(attended, (steps[1],))
    hidden = mix(attn_spots(1), block, attended, group, mix_weight)

    page_count = count // PAGE
    targets = place * page_count + jnp.arange(page_count, dtype=jnp.int32)
    table = page_table[0]
    logical = jnp.sum(
        jnp.where(
            table[None, :] == targets[:, None],
            jnp.arange(table.shape[0], dtype=jnp.int32)[None, :],
            0,
        ),
        axis=1,
    )
    first_row = logical * PAGE
    cache = qkv[:, QW:]
    kv_pages = jnp.stack(
        [lax.dynamic_slice_in_dim(cache, first_row[i], PAGE, 0) for i in range(page_count)]
    )

    span = D // (reps // 2)
    up_spots = (chip ^ jnp.arange(reps // 2, dtype=jnp.int32)) * span
    normed_two = norm_blocks(up_spots, span, hidden, moe_gain)
    other_two = across_rep(normed_two, 1)
    both_gates = jnp.concatenate([group_gates, across_rep(group_gates, 1)], axis=0)
    my_gates = lax.dynamic_slice_in_dim(both_gates, core * half_experts, half_experts, 1).astype(F32)
    chip_rows = 2 * rows_out
    whose = [chip ^ jnp.array(chip_order(n % 2), jnp.int32) for n in range(CHUNKS)]
    down_spots = [spots * chip_rows for spots in whose]
    if chip_rows % 16 != 0:
        for n, part in enumerate(down_parts):
            part = jnp.take(jnp.concatenate(part, axis=0), jnp.argsort(whose[n]), axis=0)
            part = part.transpose(1, 0, 2, 3)
            down_parts[n] = [part.reshape(1, part.shape[0], quarter, D)]

    orders, partial = [chip_order(k % 2) for k in range(per_chunk)], ()
    for n in range(CHUNKS):
        experts = slice(n * 2 * per_chunk, (n + 1) * 2 * per_chunk)
        weights = after(up_parts[n], partial)
        act = gate_up(orders, normed_two, other_two, my_gates[:, experts], weights)
        down = (down_spots[n], chip_rows, act, down_parts[n])
        if n + 1 < CHUNKS:
            partial = (down_project(*down, F32, addend=partial),)
        else:
            other = down_project(*down, BF, 1, 2, partial)
            came = across_rep(other, 1)
            mine = down_project(*down, F32, 0, 2, partial)

    def at(array, mask):
        return lax.dynamic_slice_in_dim(array, (place ^ mask) * count, count, 0).astype(F32)

    total = at(hidden, 0) + (at(mine, 0) + at(came, 0))
    for mask in range(1, cycle_size):
        part = (at(mine, mask) + at(came, mask)).astype(BF)
        total = total + across_blk(part, mask).astype(F32)
    return (total.astype(BF), kv_pages)


def solution(mesh):
    in_specs = (
        P(("rep", "blk"), None),
        P(("rep", "blk"), None),
        P(("rep", "blk"), None),
        P(None, ("rep", "blk"), None),
        P(None, ("rep", "blk"), None),
        P(),
        P(),
        P("rep", None),
        P("rep", None),
        P(("rep", "blk"), None),
        P(("rep", "blk"), None),
    )
    out_specs = (P(("rep", "blk"), None), P(("rep", "blk"), None, None))
    return jax.shard_map(body, mesh=mesh, in_specs=in_specs, out_specs=out_specs, check_vma=False)
```

```python
import functools
import math

import jax
import jax.numpy as jnp
from jax import lax
from jax.experimental import pallas as pl
from jax.experimental.pallas import tpu as pltpu
from jax.sharding import PartitionSpec as P

D = 1536
FF = 768
QH = 12
KVH = 2
HD = 128
E = 16
PAGE = 128
QW = 1536
QKV = 2048
WIDE = 512
ROWS = 256
EASE = 16
CHUNKS = 2
BF = jnp.bfloat16
F32 = jnp.float32
VMEM = 56 * 1024 * 1024


def rms_scale(values, gain):
    values = values.astype(F32)
    mean_sq = jnp.mean(values * values, axis=-1, keepdims=True)
    return values * lax.rsqrt(mean_sq + 1e-06) * gain


def rotation(position):
    half = HD // 2
    steps_all = jnp.arange(half, dtype=F32)
    frequency = jnp.exp(steps_all * (-2.0 * math.log(10000.0) / HD))
    angle = position[:, None] * frequency[None, :]
    cosine = jnp.cos(angle)
    sine = jnp.sin(angle)
    return (
        jnp.concatenate([cosine, cosine], axis=1),
        jnp.concatenate([-sine, sine], axis=1),
    )


def segment_begin(lengths, index):
    starts = jnp.cumsum(lengths) - lengths
    member = index[:, None] >= starts[None, :]
    return jnp.max(jnp.where(member, starts[None, :], 0), axis=1)


def cost(flops, bytes_accessed, transcendentals):
    return pl.CostEstimate(
        flops=flops // EASE, bytes_accessed=bytes_accessed // EASE, transcendentals=transcendentals // EASE
    )


def put(held, spots, first, block, value):
    rows = value.shape[0]
    if block % 16 != 0:
        held[pl.ds(first * block, rows), :] = value[...]
        return
    for k in range(rows // block):
        spot = pl.multiple_of(spots[first + k], block)
        held[pl.ds(spot, block), :] = value[k * block : (k + 1) * block, :]


def put_all(held, spots, block, pieces):
    first = 0
    for ref in pieces:
        for n in range(ref.shape[0]):
            put(held, spots, first, block, ref.at[n])
            first += ref.shape[1] // block


def project_kernel(pieces, block, spots, *refs):
    x_ref, cos_ref, sin_ref = refs[:3]
    out_ref, held = refs[3 + pieces :]
    step = pl.program_id(0)
    put_all(held, spots, block, refs[3 : 3 + pieces])
    result = jnp.dot(x_ref[...], held[...], preferred_element_type=F32)
    turning = (QW + KVH * HD) // HD
    for h in range(WIDE // HD):
        value = result[:, h * HD : (h + 1) * HD]
        turned = value * cos_ref[...] + pltpu.roll(value, HD // 2, 1) * sin_ref[...]
        value = jnp.where(step * (WIDE // HD) + h < turning, turned, value)
        out_ref[:, h * HD : (h + 1) * HD] = value.astype(BF)


def project(spots, block, x, cosine, sine, weights):
    count = x.shape[0]
    whole = lambda j, _: (0, 0)
    return pl.pallas_call(
        functools.partial(project_kernel, len(weights), block),
        grid_spec=pltpu.PrefetchScalarGridSpec(
            num_scalar_prefetch=1,
            grid=(QKV // WIDE,),
            in_specs=[
                pl.BlockSpec((count, D), whole),
                pl.BlockSpec((count, HD), whole),
                pl.BlockSpec((count, HD), whole),
            ]
            + [pl.BlockSpec(w.shape[:2] + (WIDE,), lambda j, _: (0, 0, j)) for w in weights],
            out_specs=pl.BlockSpec((count, WIDE), lambda j, _: (0, j)),
            scratch_shapes=[pltpu.VMEM((D, WIDE), BF)],
        ),
        out_shape=jax.ShapeDtypeStruct((count, QKV), BF),
        compiler_params=pltpu.CompilerParams(vmem_limit_bytes=VMEM),
        cost_estimate=cost(
            flops=2 * count * D * QKV, bytes_accessed=2 * D * QKV + 4 * count * D, transcendentals=0
        ),
        name="project",
    )(spots, x, cosine, sine, *weights)


def attend_kernel(q_ref, k_ref, v_ref, begin_ref, across_ref, out_ref):
    count = q_ref.shape[0]
    for first in range(0, count, ROWS):
        rows, seen = slice(first, first + ROWS), first + ROWS
        scores = lax.dot_general(
            q_ref[rows, :], k_ref[:seen, :], (((1,), (1,)), ((), ())), preferred_element_type=F32
        ) * (1.0 / math.sqrt(HD))
        across = across_ref[:, :seen]
        mine = first + lax.broadcasted_iota(jnp.int32, (ROWS, 1), 0)
        allowed = (across >= begin_ref[rows, :]) & (across <= mine)
        scores = jnp.where(allowed, scores, -1e30)
        highest = jnp.max(scores, axis=1, keepdims=True)
        weights = jnp.exp(scores - highest)
        total = jnp.sum(weights, axis=1, keepdims=True)
        mixed = jnp.dot(weights.astype(BF), v_ref[:seen, :], preferred_element_type=F32)
        out_ref[rows, :] = (mixed / total).astype(BF)


def attend(qkv, begin, index):
    count = qkv.shape[0]
    per = QH // KVH
    column = pl.BlockSpec((count, 1), lambda h: (0, 0))
    return pl.pallas_call(
        attend_kernel,
        grid=(QH,),
        in_specs=[
            pl.BlockSpec((count, HD), lambda h: (0, h)),
            pl.BlockSpec((count, HD), lambda h: (0, QH + h // per)),
            pl.BlockSpec((count, HD), lambda h: (0, QH + KVH + h // per)),
            column,
            pl.BlockSpec((1, count), lambda h: (0, 0)),
        ],
        out_specs=pl.BlockSpec((count, HD), lambda h: (0, h)),
        out_shape=jax.ShapeDtypeStruct((count, QW), BF),
        compiler_params=pltpu.CompilerParams(vmem_limit_bytes=VMEM),
        cost_estimate=cost(
            flops=4 * QH * count * count * HD,
            bytes_accessed=2 * count * (QKV + QW),
            transcendentals=QH * count * count,
        ),
        name="attend",
    )(qkv, qkv, qkv, begin[:, None], index[None, :])


def mix_kernel(pieces, block, span, spots, up_spots, x_ref, tokens_ref, gain_ref, *refs):
    hidden_ref, normed_ref, held, row = refs[pieces:]
    step, wide = pl.program_id(0), held.shape[1]
    put_all(held, spots, block, refs[:pieces])
    columns = pl.ds(pl.multiple_of(step * wide, wide), wide)
    hidden_ref[:, columns] = tokens_ref[...].astype(F32) + jnp.dot(
        x_ref[...], held[...], preferred_element_type=F32
    )

    @pl.when(step == D // wide - 1)
    def _():
        for first in range(0, hidden_ref.shape[0], 128):
            rows = slice(first, first + 128)
            value = hidden_ref[rows, :]
            mean_sq = jnp.mean(value * value, axis=1, keepdims=True)
            row[...] = (value * lax.rsqrt(mean_sq + 1e-06) * gain_ref[...]).astype(BF)
            for k in range(D // span):
                spot = pl.multiple_of(up_spots[k], span) if span % 128 == 0 else k * span
                normed_ref[rows, k * span : (k + 1) * span] = row[:, pl.ds(spot, span)]


def mix(spots, block, up_spots, span, x, tokens, weights, gain):
    count, wide = x.shape[0], D // 2
    whole = lambda j, *_: (0, 0)
    hidden, normed = pl.pallas_call(
        functools.partial(mix_kernel, len(weights), block, span),
        grid_spec=pltpu.PrefetchScalarGridSpec(
            num_scalar_prefetch=2,
            grid=(D // wide,),
            in_specs=[
                pl.BlockSpec((count, QW), whole),
                pl.BlockSpec((count, wide), lambda j, *_: (0, j)),
                pl.BlockSpec((1, D), whole),
            ]
            + [pl.BlockSpec(w.shape[:2] + (wide,), lambda j, *_: (0, 0, j)) for w in weights],
            out_specs=[pl.BlockSpec((count, D), whole)] * 2,
            scratch_shapes=[pltpu.VMEM((QW, wide), BF), pltpu.VMEM((128, D), BF)],
        ),
        out_shape=[
            jax.ShapeDtypeStruct((count, D), F32),
            jax.ShapeDtypeStruct((count, D), BF),
        ],
        compiler_params=pltpu.CompilerParams(vmem_limit_bytes=VMEM),
        cost_estimate=cost(
            flops=2 * count * D * QW, bytes_accessed=2 * D * QW + 10 * count * D, transcendentals=0
        ),
        name="mix",
    )(spots, up_spots, x, tokens, gain[None, :], *weights)
    if span % 128 != 0:
        normed = jnp.concatenate(
            [lax.dynamic_slice_in_dim(normed, up_spots[k], span, 1) for k in range(D // span)],
            axis=1,
        )
    return hidden, normed


def gate_up_kernel(orders, mine_ref, other_ref, gate_ref, *refs):
    weights, out_ref = refs[:-1], refs[-1]
    wide = weights[0].shape[1]
    width, span = wide // 4, D // len(orders[0])

    def one(x_ref):
        for p, order in enumerate(orders):
            some = len(order) // 2
            result = None
            for side in range(2):
                blocks = order[side * some : (side + 1) * some]
                if blocks == list(range(blocks[0], blocks[0] + some)):
                    x = x_ref[:, blocks[0] * span : (blocks[0] + some) * span]
                else:
                    x = jnp.concatenate(
                        [x_ref[:, k * span : (k + 1) * span] for k in blocks], axis=1
                    )
                term = jnp.dot(x, weights[2 * p + side][...], preferred_element_type=F32)
                result = term if result is None else result + term
            for e in range(2):
                n = 2 * p + e
                gate = result[:, 2 * e * width : (2 * e + 1) * width]
                up = result[:, (2 * e + 1) * width : (2 * e + 2) * width]
                activated = jnp.maximum(gate, 0.0) * up * gate_ref[:, n : n + 1]
                out_ref[:, n * width : (n + 1) * width] = activated.astype(BF)

    @pl.when(pl.program_id(0) == 0)
    def _():
        one(mine_ref)

    @pl.when(pl.program_id(0) == 1)
    def _():
        one(other_ref)


def gate_up(orders, mine, other, gate, weights):
    count, experts = mine.shape[0], gate.shape[1]
    deep, wide = weights[0].shape
    whole = pl.BlockSpec((deep, wide), lambda i: (0, 0))
    rows = pl.BlockSpec((count, D), lambda i: (0, 0))
    return pl.pallas_call(
        functools.partial(gate_up_kernel, orders),
        grid=(2,),
        in_specs=[rows, rows, pl.BlockSpec((count, experts), lambda i: (i, 0))]
        + [whole] * len(weights),
        out_specs=pl.BlockSpec((count, experts * wide // 4), lambda i: (i, 0)),
        out_shape=jax.ShapeDtypeStruct((2 * count, experts * wide // 4), BF),
        compiler_params=pltpu.CompilerParams(vmem_limit_bytes=VMEM),
        cost_estimate=cost(
            flops=2 * experts * count * D * wide,
            bytes_accessed=D * (experts * wide + 4 * count),
            transcendentals=0,
        ),
        name="gate_up",
    )(mine, other, gate, *weights)


def down_kernel(block, stacks, spots, act_ref, *refs):
    weights, held = refs[:stacks], refs[-1]
    addend, out_ref = refs[stacks:-2], refs[-2]
    experts = weights[0].shape[1]
    span = held.shape[0] // experts
    for e in range(experts):
        put_all(held.at[pl.ds(e * span, span)], spots, block, [w.at[:, e] for w in weights])
    total = jnp.dot(act_ref[...], held[...], preferred_element_type=F32)
    if addend:
        total += addend[0][...]
    out_ref[...] = total.astype(out_ref.dtype)


def down_project(spots, block, act, weights, kind, part=0, parts=1, addend=()):
    rows, deep = act.shape
    rows, wide = rows // parts, D // 2
    return pl.pallas_call(
        functools.partial(down_kernel, block, len(weights)),
        grid_spec=pltpu.PrefetchScalarGridSpec(
            num_scalar_prefetch=1,
            grid=(D // wide,),
            in_specs=[pl.BlockSpec((rows, deep), lambda j, _: (part, 0))]
            + [pl.BlockSpec(w.shape[:3] + (wide,), lambda j, _: (0, 0, 0, j)) for w in weights]
            + [pl.BlockSpec((rows, wide), lambda j, _: (part, j)) for _ in addend],
            out_specs=pl.BlockSpec((rows, wide), lambda j, _: (0, j)),
            scratch_shapes=[pltpu.VMEM((deep, wide), BF)],
        ),
        out_shape=jax.ShapeDtypeStruct((rows, D), kind),
        compiler_params=pltpu.CompilerParams(vmem_limit_bytes=VMEM),
        cost_estimate=cost(
            flops=2 * rows * D * deep,
            bytes_accessed=2 * D * deep + 2 * rows * deep + 8 * rows * D,
            transcendentals=0,
        ),
        name="down",
    )(spots, act, *weights, *addend)


def across_blk(value, mask):
    return lax.ppermute(value, "blk", [(i, i ^ mask) for i in range(lax.axis_size("blk"))])


def across_rep(value, mask):
    return lax.ppermute(value, "rep", [(i, i ^ mask) for i in range(lax.axis_size("rep"))])


def chip_bits():
    return (lax.axis_size("rep") // 2).bit_length() - 1


def chip_bits():
    return (lax.axis_size("rep") // 2).bit_length() - 1


def chip_start(value, turn):
    return value[None], across_rep(value[None], 2 << turn)


def chip_gather(held, came, turn, gate=()):
    bits = chip_bits()
    for n in range(1, bits):
        held = jnp.concatenate([held, came], axis=0)
        came = across_rep(after(held, gate), 2 << ((n + turn) % bits))
    return [held, came]


def chip_order(turn):
    bits = chip_bits()
    order = [0]
    for n in range(bits):
        order = order + [k ^ (1 << ((n + turn) % bits)) for k in order]
    return order


def after(value, other):
    if isinstance(other, tuple) and not other:
        return value
    return lax.optimization_barrier((value, other))[0]


def exchange_blk(value):
    return lax.all_to_all(value, "blk", 0, 0, tiled=True)


def gather_blk(value):
    size = lax.axis_size("blk")
    return exchange_blk(jnp.broadcast_to(value[None], (size,) + value.shape))


def body(
    tokens,
    attn_in,
    attn_out,
    expert_in,
    expert_out,
    attn_gain,
    moe_gain,
    lengths,
    page_table,
    routes,
    gates,
):
    count = tokens.shape[0]
    reps, cycle_size = lax.axis_size("rep"), lax.axis_size("blk")
    rep, place = lax.axis_index("rep"), lax.axis_index("blk")
    chip, core = rep // 2, rep % 2
    group_rows = count * cycle_size
    half_experts = E // 2
    quarter = FF // cycle_size
    rows_in, rows_out = expert_in.shape[1], expert_out.shape[1]

    def split_cores(value):
        half = value.shape[0] // 2
        mine = lax.dynamic_slice_in_dim(value, core * half, half, 0)
        other = lax.dynamic_slice_in_dim(value, (1 - core) * half, half, 0)
        came = across_rep(other, 1)
        return jnp.stack(
            [jnp.where(core == 0, mine, came), jnp.where(core == 0, came, mine)], axis=1
        )

    down = split_cores(expert_out.astype(BF)).reshape(half_experts, 2 * rows_out, D)
    down_first = [chip_start(down[n * 4 : (n + 1) * 4], n % 2) for n in range(half_experts // 4)]

    down_parts = [chip_gather(*down_first[n], n % 2) for n in range(len(down_first))]

    spot = jnp.arange(2 * FF, dtype=jnp.int32)
    inner = spot % rows_out
    from_rep = (spot // rows_out) % reps
    which = (spot // quarter) % 2
    from_blk = spot // (2 * quarter)
    column = which * FF + (from_rep * cycle_size + from_blk) * rows_out + inner
    shuffle = (spot[:, None] == column[None, :]).astype(BF)
    expert_in = after(expert_in, down_first)
    ordered = jnp.dot(
        expert_in.astype(BF).reshape(E * rows_in, 2 * FF), shuffle, preferred_element_type=F32
    )
    ordered = ordered.astype(BF).reshape(E // 2, 2, rows_in, 2 * FF)
    pairs = jnp.stack(
        [
            jnp.concatenate(
                [
                    lax.slice_in_dim(ordered[:, e], b * 2 * quarter, (b + 1) * 2 * quarter, axis=2)
                    for e in range(2)
                ],
                axis=2,
            )
            for b in range(cycle_size)
        ],
        axis=1,
    )
    pairs = split_cores(pairs)
    per_chunk = half_experts // 2 // CHUNKS

    attn_here = jnp.concatenate([attn_in.astype(BF), attn_out.astype(BF)], axis=1)
    attn_line = gather_blk(attn_here).reshape(cycle_size * rows_in, QKV + D)
    ready = after(attn_line, down_parts)
    qkv_first = chip_start(ready[:, :QKV], 0)
    mix_first = chip_start(ready[:, QKV:], 1)

    gate = (qkv_first, mix_first)
    qkv_own = chip_gather(*qkv_first, 0, gate)
    mix_own = chip_gather(*mix_first, 1, gate)
    qkv_weight = qkv_own + [across_rep(v, 1) for v in qkv_own]
    mix_weight = mix_own + [across_rep(v, 1) for v in mix_own]

    def line_up(n, earlier):
        chunk = pairs[n * per_chunk : (n + 1) * per_chunk].transpose(2, 0, 1, 3, 4)
        lined = exchange_blk(after(chunk, earlier)).transpose(1, 2, 0, 3, 4)
        return lined.reshape(per_chunk, 2 * cycle_size * rows_in, 4 * quarter)

    lines = [line_up(0, (attn_line, down_first))]

    expert_ids = jnp.arange(E, dtype=jnp.int32)
    dense = jnp.sum(
        jnp.where(
            routes[:, :, None] == expert_ids[None, None, :],
            gates.astype(F32)[:, :, None],
            F32(0.0),
        ),
        axis=1,
    ).astype(BF)
    sent = jnp.concatenate([tokens, jnp.pad(dense, ((0, 0), (0, 128 - E)))], axis=1)
    line = gather_blk(after(sent, (lines[0], qkv_first, mix_first))).reshape(group_rows, -1)
    group, group_gates = line[:, :D], line[:, D : D + E]

    for n in range(1, CHUNKS):
        lines.append(line_up(n, (line, lines[-1])))

    index = jnp.arange(group_rows, dtype=jnp.int32)
    begin = segment_begin(lengths[0], index)
    cosine, sine = rotation((index - begin).astype(F32))
    block = cycle_size * rows_in

    def attn_spots(turn):
        from_chip = chip ^ jnp.array(chip_order(turn), jnp.int32)
        from_rep = from_chip[None, :] * 2 + (core ^ jnp.arange(2, dtype=jnp.int32))[:, None]
        return (from_rep * block).reshape(-1)

    normed = rms_scale(group, attn_gain).astype(BF)
    up_parts, steps, gate = [], [], ()
    for n in range(CHUNKS):
        lined = after(lines[n], gate)
        first = [chip_start(lined[k], k % 2) for k in range(per_chunk)]
        parts = [chip_gather(*first[k], k % 2) for k in range(per_chunk)]
        up_parts.append([p.reshape(-1, 4 * quarter) for part in parts for p in part])
        steps += [first, parts]
        gate = (parts,)
        if n == 0:
            x = after(normed, (first,))
            qkv = project(attn_spots(0), block, x, cosine, sine, qkv_weight)
            attended = attend(qkv, begin, index)
            gate = (attended,)
    attended = after(attended, (steps[1],))
    span = D // (reps // 2)
    up_spots = (chip ^ jnp.arange(reps // 2, dtype=jnp.int32)) * span
    hidden, normed_two = mix(
        attn_spots(1), block, up_spots, span, attended, group, mix_weight, moe_gain
    )

    page_count = count // PAGE
    targets = place * page_count + jnp.arange(page_count, dtype=jnp.int32)
    table = page_table[0]
    logical = jnp.sum(
        jnp.where(
            table[None, :] == targets[:, None],
            jnp.arange(table.shape[0], dtype=jnp.int32)[None, :],
            0,
        ),
        axis=1,
    )
    first_row = logical * PAGE
    cache = qkv[:, QW:]
    kv_pages = jnp.stack(
        [lax.dynamic_slice_in_dim(cache, first_row[i], PAGE, 0) for i in range(page_count)]
    )

    other_two = across_rep(normed_two, 1)
    both_gates = jnp.concatenate([group_gates, across_rep(group_gates, 1)], axis=0)
    my_gates = lax.dynamic_slice_in_dim(both_gates, core * half_experts, half_experts, 1).astype(F32)
    chip_rows = 2 * rows_out
    whose = [chip ^ jnp.array(chip_order(n % 2), jnp.int32) for n in range(CHUNKS)]
    down_spots = [spots * chip_rows for spots in whose]
    if chip_rows % 16 != 0:
        for n, part in enumerate(down_parts):
            part = jnp.take(jnp.concatenate(part, axis=0), jnp.argsort(whose[n]), axis=0)
            part = part.transpose(1, 0, 2, 3)
            down_parts[n] = [part.reshape(1, part.shape[0], quarter, D)]

    orders, partial = [chip_order(k % 2) for k in range(per_chunk)], ()
    for n in range(CHUNKS):
        experts = slice(n * 2 * per_chunk, (n + 1) * 2 * per_chunk)
        weights = after(up_parts[n], partial)
        act = gate_up(orders, normed_two, other_two, my_gates[:, experts], weights)
        down = (down_spots[n], chip_rows, act, down_parts[n])
        if n + 1 < CHUNKS:
            partial = (down_project(*down, F32, addend=partial),)
        else:
            other = down_project(*down, BF, 1, 2, partial)
            came = across_rep(other, 1)
            mine = down_project(*down, F32, 0, 2, partial)

    def at(array, mask):
        return lax.dynamic_slice_in_dim(array, (place ^ mask) * count, count, 0).astype(F32)

    total = at(hidden, 0) + (at(mine, 0) + at(came, 0))
    for mask in range(1, cycle_size):
        part = (at(mine, mask) + at(came, mask)).astype(BF)
        total = total + across_blk(part, mask).astype(F32)
    return (total.astype(BF), kv_pages)


def solution(mesh):
    in_specs = (
        P(("rep", "blk"), None),
        P(("rep", "blk"), None),
        P(("rep", "blk"), None),
        P(None, ("rep", "blk"), None),
        P(None, ("rep", "blk"), None),
        P(),
        P(),
        P("rep", None),
        P("rep", None),
        P(("rep", "blk"), None),
        P(("rep", "blk"), None),
    )
    out_specs = (P(("rep", "blk"), None), P(("rep", "blk"), None, None))
    return jax.shard_map(body, mesh=mesh, in_specs=in_specs, out_specs=out_specs, check_vma=False)
```

```python
import functools
import math

import jax
import jax.numpy as jnp
from jax import lax
from jax.experimental import pallas as pl
from jax.experimental.pallas import tpu as pltpu
from jax.sharding import PartitionSpec as P

D = 1536
FF = 768
QH = 12
KVH = 2
HD = 128
E = 16
PAGE = 128
QW = 1536
QKV = 2048
WIDE = 1024
ROWS = 256
EASE = 16
CHUNKS = 2
BF = jnp.bfloat16
F32 = jnp.float32
VMEM = 56 * 1024 * 1024


def rms_scale(values, gain):
    values = values.astype(F32)
    mean_sq = jnp.mean(values * values, axis=-1, keepdims=True)
    return values * lax.rsqrt(mean_sq + 1e-06) * gain


def rotation(position):
    half = HD // 2
    steps_all = jnp.arange(half, dtype=F32)
    frequency = jnp.exp(steps_all * (-2.0 * math.log(10000.0) / HD))
    angle = position[:, None] * frequency[None, :]
    cosine = jnp.cos(angle)
    sine = jnp.sin(angle)
    return (
        jnp.concatenate([cosine, cosine], axis=1),
        jnp.concatenate([-sine, sine], axis=1),
    )


def segment_begin(lengths, index):
    starts = jnp.cumsum(lengths) - lengths
    member = index[:, None] >= starts[None, :]
    return jnp.max(jnp.where(member, starts[None, :], 0), axis=1)


def cost(flops, bytes_accessed, transcendentals):
    return pl.CostEstimate(
        flops=flops // EASE, bytes_accessed=bytes_accessed // EASE, transcendentals=transcendentals // EASE
    )


def put(held, spots, first, block, value):
    rows = value.shape[0]
    if block % 16 != 0:
        held[pl.ds(first * block, rows), :] = value[...]
        return
    for k in range(rows // block):
        spot = pl.multiple_of(spots[first + k], block)
        held[pl.ds(spot, block), :] = value[k * block : (k + 1) * block, :]


def put_all(held, spots, block, pieces):
    first = 0
    for ref in pieces:
        for n in range(ref.shape[0]):
            put(held, spots, first, block, ref.at[n])
            first += ref.shape[1] // block


def project_kernel(pieces, block, spots, *refs):
    x_ref, cos_ref, sin_ref = refs[:3]
    out_ref, held = refs[3 + pieces :]
    step = pl.program_id(0)
    put_all(held, spots, block, refs[3 : 3 + pieces])
    result = jnp.dot(x_ref[...], held[...], preferred_element_type=F32)
    turning = (QW + KVH * HD) // HD
    for h in range(WIDE // HD):
        value = result[:, h * HD : (h + 1) * HD]
        turned = value * cos_ref[...] + pltpu.roll(value, HD // 2, 1) * sin_ref[...]
        value = jnp.where(step * (WIDE // HD) + h < turning, turned, value)
        out_ref[:, h * HD : (h + 1) * HD] = value.astype(BF)


def project(spots, block, x, cosine, sine, weights):
    count = x.shape[0]
    whole = lambda j, _: (0, 0)
    return pl.pallas_call(
        functools.partial(project_kernel, len(weights), block),
        grid_spec=pltpu.PrefetchScalarGridSpec(
            num_scalar_prefetch=1,
            grid=(QKV // WIDE,),
            in_specs=[
                pl.BlockSpec((count, D), whole),
                pl.BlockSpec((count, HD), whole),
                pl.BlockSpec((count, HD), whole),
            ]
            + [pl.BlockSpec(w.shape[:2] + (WIDE,), lambda j, _: (0, 0, j)) for w in weights],
            out_specs=pl.BlockSpec((count, WIDE), lambda j, _: (0, j)),
            scratch_shapes=[pltpu.VMEM((D, WIDE), BF)],
        ),
        out_shape=jax.ShapeDtypeStruct((count, QKV), BF),
        compiler_params=pltpu.CompilerParams(vmem_limit_bytes=VMEM),
        cost_estimate=cost(
            flops=2 * count * D * QKV, bytes_accessed=2 * D * QKV + 4 * count * D, transcendentals=0
        ),
        name="project",
    )(spots, x, cosine, sine, *weights)


def attend_kernel(q_ref, k_ref, v_ref, begin_ref, across_ref, out_ref):
    count = q_ref.shape[0]
    for first, h in [(f, h) for f in range(0, count, ROWS) for h in range(2)]:
        rows, seen = slice(first, first + ROWS), first + ROWS
        head = slice(h * HD, (h + 1) * HD)
        scores = lax.dot_general(
            q_ref[rows, head], k_ref[:seen, :], (((1,), (1,)), ((), ())), preferred_element_type=F32
        ) * (1.0 / math.sqrt(HD))
        across = across_ref[:, :seen]
        mine = first + lax.broadcasted_iota(jnp.int32, (ROWS, 1), 0)
        allowed = (across >= begin_ref[rows, :]) & (across <= mine)
        scores = jnp.where(allowed, scores, -1e30)
        highest = jnp.max(scores, axis=1, keepdims=True)
        weights = jnp.exp(scores - highest)
        total = jnp.sum(weights, axis=1, keepdims=True)
        mixed = jnp.dot(weights.astype(BF), v_ref[:seen, :], preferred_element_type=F32)
        out_ref[rows, head] = (mixed / total).astype(BF)


def attend(qkv, begin, index):
    count = qkv.shape[0]
    per = QH // KVH
    column = pl.BlockSpec((count, 1), lambda h: (0, 0))
    return pl.pallas_call(
        attend_kernel,
        grid=(QH // 2,),
        in_specs=[
            pl.BlockSpec((count, 2 * HD), lambda h: (0, h)),
            pl.BlockSpec((count, HD), lambda h: (0, QH + 2 * h // per)),
            pl.BlockSpec((count, HD), lambda h: (0, QH + KVH + 2 * h // per)),
            column,
            pl.BlockSpec((1, count), lambda h: (0, 0)),
        ],
        out_specs=pl.BlockSpec((count, 2 * HD), lambda h: (0, h)),
        out_shape=jax.ShapeDtypeStruct((count, QW), BF),
        compiler_params=pltpu.CompilerParams(vmem_limit_bytes=VMEM),
        cost_estimate=cost(
            flops=4 * QH * count * count * HD,
            bytes_accessed=2 * count * (QKV + QW),
            transcendentals=QH * count * count,
        ),
        name="attend",
    )(qkv, qkv, qkv, begin[:, None], index[None, :])


def mix_kernel(pieces, block, span, spots, up_spots, x_ref, tokens_ref, gain_ref, *refs):
    hidden_ref, normed_ref, held, row = refs[pieces:]
    step, wide = pl.program_id(0), held.shape[1]
    put_all(held, spots, block, refs[:pieces])
    columns = pl.ds(pl.multiple_of(step * wide, wide), wide)
    hidden_ref[:, columns] = tokens_ref[...].astype(F32) + jnp.dot(
        x_ref[...], held[...], preferred_element_type=F32
    )

    @pl.when(step == D // wide - 1)
    def _():
        for first in range(0, hidden_ref.shape[0], 128):
            rows = slice(first, first + 128)
            value = hidden_ref[rows, :]
            mean_sq = jnp.mean(value * value, axis=1, keepdims=True)
            row[...] = (value * lax.rsqrt(mean_sq + 1e-06) * gain_ref[...]).astype(BF)
            for k in range(D // span):
                spot = pl.multiple_of(up_spots[k], span) if span % 128 == 0 else k * span
                normed_ref[rows, k * span : (k + 1) * span] = row[:, pl.ds(spot, span)]


def mix(spots, block, up_spots, span, x, tokens, weights, gain):
    count, wide = x.shape[0], D // 2
    whole = lambda j, *_: (0, 0)
    hidden, normed = pl.pallas_call(
        functools.partial(mix_kernel, len(weights), block, span),
        grid_spec=pltpu.PrefetchScalarGridSpec(
            num_scalar_prefetch=2,
            grid=(D // wide,),
            in_specs=[
                pl.BlockSpec((count, QW), whole),
                pl.BlockSpec((count, wide), lambda j, *_: (0, j)),
                pl.BlockSpec((1, D), whole),
            ]
            + [pl.BlockSpec(w.shape[:2] + (wide,), lambda j, *_: (0, 0, j)) for w in weights],
            out_specs=[pl.BlockSpec((count, D), whole)] * 2,
            scratch_shapes=[pltpu.VMEM((QW, wide), BF), pltpu.VMEM((128, D), BF)],
        ),
        out_shape=[
            jax.ShapeDtypeStruct((count, D), F32),
            jax.ShapeDtypeStruct((count, D), BF),
        ],
        compiler_params=pltpu.CompilerParams(vmem_limit_bytes=VMEM),
        cost_estimate=cost(
            flops=2 * count * D * QW, bytes_accessed=2 * D * QW + 10 * count * D, transcendentals=0
        ),
        name="mix",
    )(spots, up_spots, x, tokens, gain[None, :], *weights)
    if span % 128 != 0:
        normed = jnp.concatenate(
            [lax.dynamic_slice_in_dim(normed, up_spots[k], span, 1) for k in range(D // span)],
            axis=1,
        )
    return hidden, normed


def gate_up_kernel(orders, mine_ref, other_ref, gate_ref, *refs):
    weights, out_ref = refs[:-1], refs[-1]
    wide = weights[0].shape[1]
    width, span = wide // 4, D // len(orders[0])

    def one(x_ref):
        for p, order in enumerate(orders):
            some = len(order) // 2
            result = None
            for side in range(2):
                blocks = order[side * some : (side + 1) * some]
                if blocks == list(range(blocks[0], blocks[0] + some)):
                    x = x_ref[:, blocks[0] * span : (blocks[0] + some) * span]
                else:
                    x = jnp.concatenate(
                        [x_ref[:, k * span : (k + 1) * span] for k in blocks], axis=1
                    )
                term = jnp.dot(x, weights[2 * p + side][...], preferred_element_type=F32)
                result = term if result is None else result + term
            for e in range(2):
                n = 2 * p + e
                gate = result[:, 2 * e * width : (2 * e + 1) * width]
                up = result[:, (2 * e + 1) * width : (2 * e + 2) * width]
                activated = jnp.maximum(gate, 0.0) * up * gate_ref[:, n : n + 1]
                out_ref[:, n * width : (n + 1) * width] = activated.astype(BF)

    @pl.when(pl.program_id(0) == 0)
    def _():
        one(mine_ref)

    @pl.when(pl.program_id(0) == 1)
    def _():
        one(other_ref)


def gate_up(orders, mine, other, gate, weights):
    count, experts = mine.shape[0], gate.shape[1]
    deep, wide = weights[0].shape
    whole = pl.BlockSpec((deep, wide), lambda i: (0, 0))
    rows = pl.BlockSpec((count, D), lambda i: (0, 0))
    return pl.pallas_call(
        functools.partial(gate_up_kernel, orders),
        grid=(2,),
        in_specs=[rows, rows, pl.BlockSpec((count, experts), lambda i: (i, 0))]
        + [whole] * len(weights),
        out_specs=pl.BlockSpec((count, experts * wide // 4), lambda i: (i, 0)),
        out_shape=jax.ShapeDtypeStruct((2 * count, experts * wide // 4), BF),
        compiler_params=pltpu.CompilerParams(vmem_limit_bytes=VMEM),
        cost_estimate=cost(
            flops=2 * experts * count * D * wide,
            bytes_accessed=D * (experts * wide + 4 * count),
            transcendentals=0,
        ),
        name="gate_up",
    )(mine, other, gate, *weights)


def down_kernel(block, stacks, spots, act_ref, *refs):
    weights, held = refs[:stacks], refs[-1]
    addend, out_ref = refs[stacks:-2], refs[-2]
    experts = weights[0].shape[1]
    span = held.shape[0] // experts
    for e in range(experts):
        put_all(held.at[pl.ds(e * span, span)], spots, block, [w.at[:, e] for w in weights])
    total = jnp.dot(act_ref[...], held[...], preferred_element_type=F32)
    if addend:
        total += addend[0][...]
    out_ref[...] = total.astype(out_ref.dtype)


def down_project(spots, block, act, weights, kind, part=0, parts=1, addend=()):
    rows, deep = act.shape
    rows, wide = rows // parts, D // 2
    return pl.pallas_call(
        functools.partial(down_kernel, block, len(weights)),
        grid_spec=pltpu.PrefetchScalarGridSpec(
            num_scalar_prefetch=1,
            grid=(D // wide,),
            in_specs=[pl.BlockSpec((rows, deep), lambda j, _: (part, 0))]
            + [pl.BlockSpec(w.shape[:3] + (wide,), lambda j, _: (0, 0, 0, j)) for w in weights]
            + [pl.BlockSpec((rows, wide), lambda j, _: (part, j)) for _ in addend],
            out_specs=pl.BlockSpec((rows, wide), lambda j, _: (0, j)),
            scratch_shapes=[pltpu.VMEM((deep, wide), BF)],
        ),
        out_shape=jax.ShapeDtypeStruct((rows, D), kind),
        compiler_params=pltpu.CompilerParams(vmem_limit_bytes=VMEM),
        cost_estimate=cost(
            flops=2 * rows * D * deep,
            bytes_accessed=2 * D * deep + 2 * rows * deep + 8 * rows * D,
            transcendentals=0,
        ),
        name="down",
    )(spots, act, *weights, *addend)


def across_blk(value, mask):
    return lax.ppermute(value, "blk", [(i, i ^ mask) for i in range(lax.axis_size("blk"))])


def across_rep(value, mask):
    return lax.ppermute(value, "rep", [(i, i ^ mask) for i in range(lax.axis_size("rep"))])


def chip_bits():
    return (lax.axis_size("rep") // 2).bit_length() - 1


def chip_bits():
    return (lax.axis_size("rep") // 2).bit_length() - 1


def chip_start(value, turn):
    return value[None], across_rep(value[None], 2 << turn)


def chip_gather(held, came, turn, gate=()):
    bits = chip_bits()
    for n in range(1, bits):
        held = jnp.concatenate([held, came], axis=0)
        came = across_rep(after(held, gate), 2 << ((n + turn) % bits))
    return [held, came]


def chip_order(turn):
    bits = chip_bits()
    order = [0]
    for n in range(bits):
        order = order + [k ^ (1 << ((n + turn) % bits)) for k in order]
    return order


def after(value, other):
    if isinstance(other, tuple) and not other:
        return value
    return lax.optimization_barrier((value, other))[0]


def exchange_blk(value):
    return lax.all_to_all(value, "blk", 0, 0, tiled=True)


def gather_blk(value):
    size = lax.axis_size("blk")
    return exchange_blk(jnp.broadcast_to(value[None], (size,) + value.shape))


def body(
    tokens,
    attn_in,
    attn_out,
    expert_in,
    expert_out,
    attn_gain,
    moe_gain,
    lengths,
    page_table,
    routes,
    gates,
):
    count = tokens.shape[0]
    reps, cycle_size = lax.axis_size("rep"), lax.axis_size("blk")
    rep, place = lax.axis_index("rep"), lax.axis_index("blk")
    chip, core = rep // 2, rep % 2
    group_rows = count * cycle_size
    half_experts = E // 2
    quarter = FF // cycle_size
    rows_in, rows_out = expert_in.shape[1], expert_out.shape[1]

    def split_cores(value):
        half = value.shape[0] // 2
        mine = lax.dynamic_slice_in_dim(value, core * half, half, 0)
        other = lax.dynamic_slice_in_dim(value, (1 - core) * half, half, 0)
        came = across_rep(other, 1)
        return jnp.stack(
            [jnp.where(core == 0, mine, came), jnp.where(core == 0, came, mine)], axis=1
        )

    down = split_cores(expert_out.astype(BF)).reshape(half_experts, 2 * rows_out, D)
    down_first = [chip_start(down[n * 4 : (n + 1) * 4], n % 2) for n in range(half_experts // 4)]

    down_parts = [chip_gather(*down_first[n], n % 2) for n in range(len(down_first))]

    spot = jnp.arange(2 * FF, dtype=jnp.int32)
    inner = spot % rows_out
    from_rep = (spot // rows_out) % reps
    which = (spot // quarter) % 2
    from_blk = spot // (2 * quarter)
    column = which * FF + (from_rep * cycle_size + from_blk) * rows_out + inner
    shuffle = (spot[:, None] == column[None, :]).astype(BF)
    expert_in = after(expert_in, down_first)
    ordered = jnp.dot(
        expert_in.astype(BF).reshape(E * rows_in, 2 * FF), shuffle, preferred_element_type=F32
    )
    ordered = ordered.astype(BF).reshape(E // 2, 2, rows_in, 2 * FF)
    pairs = jnp.stack(
        [
            jnp.concatenate(
                [
                    lax.slice_in_dim(ordered[:, e], b * 2 * quarter, (b + 1) * 2 * quarter, axis=2)
                    for e in range(2)
                ],
                axis=2,
            )
            for b in range(cycle_size)
        ],
        axis=1,
    )
    pairs = split_cores(pairs)
    per_chunk = half_experts // 2 // CHUNKS

    attn_here = jnp.concatenate([attn_in.astype(BF), attn_out.astype(BF)], axis=1)
    attn_line = gather_blk(attn_here).reshape(cycle_size * rows_in, QKV + D)
    ready = after(attn_line, down_parts)
    qkv_first = chip_start(ready[:, :QKV], 0)
    mix_first = chip_start(ready[:, QKV:], 1)

    gate = (qkv_first, mix_first)
    qkv_own = chip_gather(*qkv_first, 0, gate)
    mix_own = chip_gather(*mix_first, 1, gate)
    qkv_weight = qkv_own + [across_rep(v, 1) for v in qkv_own]
    mix_weight = mix_own + [across_rep(v, 1) for v in mix_own]

    def line_up(n, earlier):
        chunk = pairs[n * per_chunk : (n + 1) * per_chunk].transpose(2, 0, 1, 3, 4)
        lined = exchange_blk(after(chunk, earlier)).transpose(1, 2, 0, 3, 4)
        return lined.reshape(per_chunk, 2 * cycle_size * rows_in, 4 * quarter)

    lines = [line_up(0, (attn_line, down_first))]

    expert_ids = jnp.arange(E, dtype=jnp.int32)
    dense = jnp.sum(
        jnp.where(
            routes[:, :, None] == expert_ids[None, None, :],
            gates.astype(F32)[:, :, None],
            F32(0.0),
        ),
        axis=1,
    ).astype(BF)
    sent = jnp.concatenate([tokens, jnp.pad(dense, ((0, 0), (0, 128 - E)))], axis=1)
    line = gather_blk(after(sent, (lines[0], qkv_first, mix_first))).reshape(group_rows, -1)
    group, group_gates = line[:, :D], line[:, D : D + E]

    for n in range(1, CHUNKS):
        lines.append(line_up(n, (line, lines[-1])))

    index = jnp.arange(group_rows, dtype=jnp.int32)
    begin = segment_begin(lengths[0], index)
    cosine, sine = rotation((index - begin).astype(F32))
    block = cycle_size * rows_in

    def attn_spots(turn):
        from_chip = chip ^ jnp.array(chip_order(turn), jnp.int32)
        from_rep = from_chip[None, :] * 2 + (core ^ jnp.arange(2, dtype=jnp.int32))[:, None]
        return (from_rep * block).reshape(-1)

    normed = rms_scale(group, attn_gain).astype(BF)
    up_parts, steps, gate = [], [], ()
    for n in range(CHUNKS):
        lined = after(lines[n], gate)
        first = [chip_start(lined[k], k % 2) for k in range(per_chunk)]
        parts = [chip_gather(*first[k], k % 2) for k in range(per_chunk)]
        up_parts.append([p.reshape(-1, 4 * quarter) for part in parts for p in part])
        steps += [first, parts]
        gate = (parts,)
        if n == 0:
            x = after(normed, (first,))
            qkv = project(attn_spots(0), block, x, cosine, sine, qkv_weight)
            attended = attend(qkv, begin, index)
            gate = (attended,)
    attended = after(attended, (steps[1],))
    span = D // (reps // 2)
    up_spots = (chip ^ jnp.arange(reps // 2, dtype=jnp.int32)) * span
    hidden, normed_two = mix(
        attn_spots(1), block, up_spots, span, attended, group, mix_weight, moe_gain
    )

    page_count = count // PAGE
    targets = place * page_count + jnp.arange(page_count, dtype=jnp.int32)
    table = page_table[0]
    logical = jnp.sum(
        jnp.where(
            table[None, :] == targets[:, None],
            jnp.arange(table.shape[0], dtype=jnp.int32)[None, :],
            0,
        ),
        axis=1,
    )
    first_row = logical * PAGE
    cache = qkv[:, QW:]
    kv_pages = jnp.stack(
        [lax.dynamic_slice_in_dim(cache, first_row[i], PAGE, 0) for i in range(page_count)]
    )

    other_two = across_rep(normed_two, 1)
    both_gates = jnp.concatenate([group_gates, across_rep(group_gates, 1)], axis=0)
    my_gates = lax.dynamic_slice_in_dim(both_gates, core * half_experts, half_experts, 1).astype(F32)
    chip_rows = 2 * rows_out
    whose = [chip ^ jnp.array(chip_order(n % 2), jnp.int32) for n in range(CHUNKS)]
    down_spots = [spots * chip_rows for spots in whose]
    if chip_rows % 16 != 0:
        for n, part in enumerate(down_parts):
            part = jnp.take(jnp.concatenate(part, axis=0), jnp.argsort(whose[n]), axis=0)
            part = part.transpose(1, 0, 2, 3)
            down_parts[n] = [part.reshape(1, part.shape[0], quarter, D)]

    orders, partial = [chip_order(k % 2) for k in range(per_chunk)], ()
    for n in range(CHUNKS):
        experts = slice(n * 2 * per_chunk, (n + 1) * 2 * per_chunk)
        weights = after(up_parts[n], partial)
        act = gate_up(orders, normed_two, other_two, my_gates[:, experts], weights)
        down = (down_spots[n], chip_rows, act, down_parts[n])
        if n + 1 < CHUNKS:
            partial = (down_project(*down, F32, addend=partial),)
        else:
            other = down_project(*down, BF, 1, 2, partial)
            came = across_rep(other, 1)
            mine = down_project(*down, F32, 0, 2, partial)

    def at(array, mask):
        return lax.dynamic_slice_in_dim(array, (place ^ mask) * count, count, 0).astype(F32)

    total = at(hidden, 0) + (at(mine, 0) + at(came, 0))
    for mask in range(1, cycle_size):
        part = (at(mine, mask) + at(came, mask)).astype(BF)
        total = total + across_blk(part, mask).astype(F32)
    return (total.astype(BF), kv_pages)


def solution(mesh):
    in_specs = (
        P(("rep", "blk"), None),
        P(("rep", "blk"), None),
        P(("rep", "blk"), None),
        P(None, ("rep", "blk"), None),
        P(None, ("rep", "blk"), None),
        P(),
        P(),
        P("rep", None),
        P("rep", None),
        P(("rep", "blk"), None),
        P(("rep", "blk"), None),
    )
    out_specs = (P(("rep", "blk"), None), P(("rep", "blk"), None, None))
    return jax.shard_map(body, mesh=mesh, in_specs=in_specs, out_specs=out_specs, check_vma=False)
```

```python
import functools
import math

import jax
import jax.numpy as jnp
from jax import lax
from jax.experimental import pallas as pl
from jax.experimental.pallas import tpu as pltpu
from jax.sharding import PartitionSpec as P

D = 1536
FF = 768
QH = 12
KVH = 2
HD = 128
E = 16
PAGE = 128
QW = 1536
QKV = 2048
WIDE = 1024
ROWS = 256
EASE = 16
CHUNKS = 2
BF = jnp.bfloat16
F32 = jnp.float32
VMEM = 56 * 1024 * 1024


def rms_scale(values, gain):
    values = values.astype(F32)
    mean_sq = jnp.mean(values * values, axis=-1, keepdims=True)
    return values * lax.rsqrt(mean_sq + 1e-06) * gain


def rotation(position):
    half = HD // 2
    steps_all = jnp.arange(half, dtype=F32)
    frequency = jnp.exp(steps_all * (-2.0 * math.log(10000.0) / HD))
    angle = position[:, None] * frequency[None, :]
    cosine = jnp.cos(angle)
    sine = jnp.sin(angle)
    return (
        jnp.concatenate([cosine, cosine], axis=1),
        jnp.concatenate([-sine, sine], axis=1),
    )


def segment_begin(lengths, index):
    starts = jnp.cumsum(lengths) - lengths
    member = index[:, None] >= starts[None, :]
    return jnp.max(jnp.where(member, starts[None, :], 0), axis=1)


def cost(flops, bytes_accessed, transcendentals):
    return pl.CostEstimate(
        flops=flops // EASE, bytes_accessed=bytes_accessed // EASE, transcendentals=transcendentals // EASE
    )


def put(held, spots, first, block, value):
    rows = value.shape[0]
    if block % 16 != 0:
        held[pl.ds(first * block, rows), :] = value[...]
        return
    for k in range(rows // block):
        spot = pl.multiple_of(spots[first + k], block)
        held[pl.ds(spot, block), :] = value[k * block : (k + 1) * block, :]


def put_all(held, spots, block, pieces):
    first = 0
    for ref in pieces:
        for n in range(ref.shape[0]):
            put(held, spots, first, block, ref.at[n])
            first += ref.shape[1] // block


def project_kernel(pieces, block, spots, *refs):
    x_ref, cos_ref, sin_ref = refs[:3]
    out_ref, held = refs[3 + pieces :]
    step = pl.program_id(0)
    put_all(held, spots, block, refs[3 : 3 + pieces])
    result = jnp.dot(x_ref[...], held[...], preferred_element_type=F32)
    turning = (QW + KVH * HD) // HD
    for h in range(WIDE // HD):
        value = result[:, h * HD : (h + 1) * HD]
        turned = value * cos_ref[...] + pltpu.roll(value, HD // 2, 1) * sin_ref[...]
        value = jnp.where(step * (WIDE // HD) + h < turning, turned, value)
        out_ref[:, h * HD : (h + 1) * HD] = value.astype(BF)


def project(spots, block, x, cosine, sine, weights):
    count = x.shape[0]
    whole = lambda j, _: (0, 0)
    return pl.pallas_call(
        functools.partial(project_kernel, len(weights), block),
        grid_spec=pltpu.PrefetchScalarGridSpec(
            num_scalar_prefetch=1,
            grid=(QKV // WIDE,),
            in_specs=[
                pl.BlockSpec((count, D), whole),
                pl.BlockSpec((count, HD), whole),
                pl.BlockSpec((count, HD), whole),
            ]
            + [pl.BlockSpec(w.shape[:2] + (WIDE,), lambda j, _: (0, 0, j)) for w in weights],
            out_specs=pl.BlockSpec((count, WIDE), lambda j, _: (0, j)),
            scratch_shapes=[pltpu.VMEM((D, WIDE), BF)],
        ),
        out_shape=jax.ShapeDtypeStruct((count, QKV), BF),
        compiler_params=pltpu.CompilerParams(vmem_limit_bytes=VMEM),
        cost_estimate=cost(
            flops=2 * count * D * QKV, bytes_accessed=2 * D * QKV + 4 * count * D, transcendentals=0
        ),
        name="project",
    )(spots, x, cosine, sine, *weights)


def attend_kernel(q_ref, k_ref, v_ref, begin_ref, across_ref, out_ref):
    count = q_ref.shape[0]
    for first, h in [(f, h) for f in range(0, count, ROWS) for h in range(3)]:
        rows, seen = slice(first, first + ROWS), first + ROWS
        head = slice(h * HD, (h + 1) * HD)
        scores = lax.dot_general(
            q_ref[rows, head], k_ref[:seen, :], (((1,), (1,)), ((), ())), preferred_element_type=F32
        ) * (1.0 / math.sqrt(HD))
        across = across_ref[:, :seen]
        mine = first + lax.broadcasted_iota(jnp.int32, (ROWS, 1), 0)
        allowed = (across >= begin_ref[rows, :]) & (across <= mine)
        scores = jnp.where(allowed, scores, -1e30)
        highest = jnp.max(scores, axis=1, keepdims=True)
        weights = jnp.exp(scores - highest)
        total = jnp.sum(weights, axis=1, keepdims=True)
        mixed = jnp.dot(weights.astype(BF), v_ref[:seen, :], preferred_element_type=F32)
        out_ref[rows, head] = (mixed / total).astype(BF)


def attend(qkv, begin, index):
    count = qkv.shape[0]
    per = QH // KVH
    column = pl.BlockSpec((count, 1), lambda h: (0, 0))
    return pl.pallas_call(
        attend_kernel,
        grid=(QH // 3,),
        in_specs=[
            pl.BlockSpec((count, 3 * HD), lambda h: (0, h)),
            pl.BlockSpec((count, HD), lambda h: (0, QH + 3 * h // per)),
            pl.BlockSpec((count, HD), lambda h: (0, QH + KVH + 3 * h // per)),
            column,
            pl.BlockSpec((1, count), lambda h: (0, 0)),
        ],
        out_specs=pl.BlockSpec((count, 3 * HD), lambda h: (0, h)),
        out_shape=jax.ShapeDtypeStruct((count, QW), BF),
        compiler_params=pltpu.CompilerParams(vmem_limit_bytes=VMEM),
        cost_estimate=cost(
            flops=4 * QH * count * count * HD,
            bytes_accessed=2 * count * (QKV + QW),
            transcendentals=QH * count * count,
        ),
        name="attend",
    )(qkv, qkv, qkv, begin[:, None], index[None, :])


def mix_kernel(pieces, block, span, spots, up_spots, x_ref, tokens_ref, gain_ref, *refs):
    hidden_ref, normed_ref, held, row = refs[pieces:]
    step, wide = pl.program_id(0), held.shape[1]
    put_all(held, spots, block, refs[:pieces])
    columns = pl.ds(pl.multiple_of(step * wide, wide), wide)
    hidden_ref[:, columns] = tokens_ref[...].astype(F32) + jnp.dot(
        x_ref[...], held[...], preferred_element_type=F32
    )

    @pl.when(step == D // wide - 1)
    def _():
        for first in range(0, hidden_ref.shape[0], 128):
            rows = slice(first, first + 128)
            value = hidden_ref[rows, :]
            mean_sq = jnp.mean(value * value, axis=1, keepdims=True)
            row[...] = (value * lax.rsqrt(mean_sq + 1e-06) * gain_ref[...]).astype(BF)
            for k in range(D // span):
                spot = pl.multiple_of(up_spots[k], span) if span % 128 == 0 else k * span
                normed_ref[rows, k * span : (k + 1) * span] = row[:, pl.ds(spot, span)]


def mix(spots, block, up_spots, span, x, tokens, weights, gain):
    count, wide = x.shape[0], D // 2
    whole = lambda j, *_: (0, 0)
    hidden, normed = pl.pallas_call(
        functools.partial(mix_kernel, len(weights), block, span),
        grid_spec=pltpu.PrefetchScalarGridSpec(
            num_scalar_prefetch=2,
            grid=(D // wide,),
            in_specs=[
                pl.BlockSpec((count, QW), whole),
                pl.BlockSpec((count, wide), lambda j, *_: (0, j)),
                pl.BlockSpec((1, D), whole),
            ]
            + [pl.BlockSpec(w.shape[:2] + (wide,), lambda j, *_: (0, 0, j)) for w in weights],
            out_specs=[pl.BlockSpec((count, D), whole)] * 2,
            scratch_shapes=[pltpu.VMEM((QW, wide), BF), pltpu.VMEM((128, D), BF)],
        ),
        out_shape=[
            jax.ShapeDtypeStruct((count, D), F32),
            jax.ShapeDtypeStruct((count, D), BF),
        ],
        compiler_params=pltpu.CompilerParams(vmem_limit_bytes=VMEM),
        cost_estimate=cost(
            flops=2 * count * D * QW, bytes_accessed=2 * D * QW + 10 * count * D, transcendentals=0
        ),
        name="mix",
    )(spots, up_spots, x, tokens, gain[None, :], *weights)
    if span % 128 != 0:
        normed = jnp.concatenate(
            [lax.dynamic_slice_in_dim(normed, up_spots[k], span, 1) for k in range(D // span)],
            axis=1,
        )
    return hidden, normed


def gate_up_kernel(orders, mine_ref, other_ref, gate_ref, *refs):
    weights, out_ref = refs[:-1], refs[-1]
    wide = weights[0].shape[1]
    width, span = wide // 4, D // len(orders[0])

    def one(x_ref):
        for p, order in enumerate(orders):
            some = len(order) // 2
            result = None
            for side in range(2):
                blocks = order[side * some : (side + 1) * some]
                if blocks == list(range(blocks[0], blocks[0] + some)):
                    x = x_ref[:, blocks[0] * span : (blocks[0] + some) * span]
                else:
                    x = jnp.concatenate(
                        [x_ref[:, k * span : (k + 1) * span] for k in blocks], axis=1
                    )
                term = jnp.dot(x, weights[2 * p + side][...], preferred_element_type=F32)
                result = term if result is None else result + term
            for e in range(2):
                n = 2 * p + e
                gate = result[:, 2 * e * width : (2 * e + 1) * width]
                up = result[:, (2 * e + 1) * width : (2 * e + 2) * width]
                activated = jnp.maximum(gate, 0.0) * up * gate_ref[:, n : n + 1]
                out_ref[:, n * width : (n + 1) * width] = activated.astype(BF)

    @pl.when(pl.program_id(0) == 0)
    def _():
        one(mine_ref)

    @pl.when(pl.program_id(0) == 1)
    def _():
        one(other_ref)


def gate_up(orders, mine, other, gate, weights):
    count, experts = mine.shape[0], gate.shape[1]
    deep, wide = weights[0].shape
    whole = pl.BlockSpec((deep, wide), lambda i: (0, 0))
    rows = pl.BlockSpec((count, D), lambda i: (0, 0))
    return pl.pallas_call(
        functools.partial(gate_up_kernel, orders),
        grid=(2,),
        in_specs=[rows, rows, pl.BlockSpec((count, experts), lambda i: (i, 0))]
        + [whole] * len(weights),
        out_specs=pl.BlockSpec((count, experts * wide // 4), lambda i: (i, 0)),
        out_shape=jax.ShapeDtypeStruct((2 * count, experts * wide // 4), BF),
        compiler_params=pltpu.CompilerParams(vmem_limit_bytes=VMEM),
        cost_estimate=cost(
            flops=2 * experts * count * D * wide,
            bytes_accessed=D * (experts * wide + 4 * count),
            transcendentals=0,
        ),
        name="gate_up",
    )(mine, other, gate, *weights)


def down_kernel(block, stacks, spots, act_ref, *refs):
    weights, held = refs[:stacks], refs[-1]
    addend, out_ref = refs[stacks:-2], refs[-2]
    experts = weights[0].shape[1]
    span = held.shape[0] // experts
    for e in range(experts):
        put_all(held.at[pl.ds(e * span, span)], spots, block, [w.at[:, e] for w in weights])
    total = jnp.dot(act_ref[...], held[...], preferred_element_type=F32)
    if addend:
        total += addend[0][...]
    out_ref[...] = total.astype(out_ref.dtype)


def down_project(spots, block, act, weights, kind, part=0, parts=1, addend=()):
    rows, deep = act.shape
    rows, wide = rows // parts, D // 2
    return pl.pallas_call(
        functools.partial(down_kernel, block, len(weights)),
        grid_spec=pltpu.PrefetchScalarGridSpec(
            num_scalar_prefetch=1,
            grid=(D // wide,),
            in_specs=[pl.BlockSpec((rows, deep), lambda j, _: (part, 0))]
            + [pl.BlockSpec(w.shape[:3] + (wide,), lambda j, _: (0, 0, 0, j)) for w in weights]
            + [pl.BlockSpec((rows, wide), lambda j, _: (part, j)) for _ in addend],
            out_specs=pl.BlockSpec((rows, wide), lambda j, _: (0, j)),
            scratch_shapes=[pltpu.VMEM((deep, wide), BF)],
        ),
        out_shape=jax.ShapeDtypeStruct((rows, D), kind),
        compiler_params=pltpu.CompilerParams(vmem_limit_bytes=VMEM),
        cost_estimate=cost(
            flops=2 * rows * D * deep,
            bytes_accessed=2 * D * deep + 2 * rows * deep + 8 * rows * D,
            transcendentals=0,
        ),
        name="down",
    )(spots, act, *weights, *addend)


def across_blk(value, mask):
    return lax.ppermute(value, "blk", [(i, i ^ mask) for i in range(lax.axis_size("blk"))])


def across_rep(value, mask):
    return lax.ppermute(value, "rep", [(i, i ^ mask) for i in range(lax.axis_size("rep"))])


def chip_bits():
    return (lax.axis_size("rep") // 2).bit_length() - 1


def chip_bits():
    return (lax.axis_size("rep") // 2).bit_length() - 1


def chip_start(value, turn):
    return value[None], across_rep(value[None], 2 << turn)


def chip_gather(held, came, turn, gate=()):
    bits = chip_bits()
    for n in range(1, bits):
        held = jnp.concatenate([held, came], axis=0)
        came = across_rep(after(held, gate), 2 << ((n + turn) % bits))
    return [held, came]


def chip_order(turn):
    bits = chip_bits()
    order = [0]
    for n in range(bits):
        order = order + [k ^ (1 << ((n + turn) % bits)) for k in order]
    return order


def after(value, other):
    if isinstance(other, tuple) and not other:
        return value
    return lax.optimization_barrier((value, other))[0]


def exchange_blk(value):
    return lax.all_to_all(value, "blk", 0, 0, tiled=True)


def gather_blk(value):
    size = lax.axis_size("blk")
    return exchange_blk(jnp.broadcast_to(value[None], (size,) + value.shape))


def body(
    tokens,
    attn_in,
    attn_out,
    expert_in,
    expert_out,
    attn_gain,
    moe_gain,
    lengths,
    page_table,
    routes,
    gates,
):
    count = tokens.shape[0]
    reps, cycle_size = lax.axis_size("rep"), lax.axis_size("blk")
    rep, place = lax.axis_index("rep"), lax.axis_index("blk")
    chip, core = rep // 2, rep % 2
    group_rows = count * cycle_size
    half_experts = E // 2
    quarter = FF // cycle_size
    rows_in, rows_out = expert_in.shape[1], expert_out.shape[1]

    def split_cores(value):
        half = value.shape[0] // 2
        mine = lax.dynamic_slice_in_dim(value, core * half, half, 0)
        other = lax.dynamic_slice_in_dim(value, (1 - core) * half, half, 0)
        came = across_rep(other, 1)
        return jnp.stack(
            [jnp.where(core == 0, mine, came), jnp.where(core == 0, came, mine)], axis=1
        )

    down = split_cores(expert_out.astype(BF)).reshape(half_experts, 2 * rows_out, D)
    down_first = [chip_start(down[n * 4 : (n + 1) * 4], n % 2) for n in range(half_experts // 4)]

    down_parts = [chip_gather(*down_first[n], n % 2) for n in range(len(down_first))]

    spot = jnp.arange(2 * FF, dtype=jnp.int32)
    inner = spot % rows_out
    from_rep = (spot // rows_out) % reps
    which = (spot // quarter) % 2
    from_blk = spot // (2 * quarter)
    column = which * FF + (from_rep * cycle_size + from_blk) * rows_out + inner
    shuffle = (spot[:, None] == column[None, :]).astype(BF)
    expert_in = after(expert_in, down_first)
    ordered = jnp.dot(
        expert_in.astype(BF).reshape(E * rows_in, 2 * FF), shuffle, preferred_element_type=F32
    )
    ordered = ordered.astype(BF).reshape(E // 2, 2, rows_in, 2 * FF)
    pairs = jnp.stack(
        [
            jnp.concatenate(
                [
                    lax.slice_in_dim(ordered[:, e], b * 2 * quarter, (b + 1) * 2 * quarter, axis=2)
                    for e in range(2)
                ],
                axis=2,
            )
            for b in range(cycle_size)
        ],
        axis=1,
    )
    pairs = split_cores(pairs)
    per_chunk = half_experts // 2 // CHUNKS

    attn_here = jnp.concatenate([attn_in.astype(BF), attn_out.astype(BF)], axis=1)
    attn_line = gather_blk(attn_here).reshape(cycle_size * rows_in, QKV + D)
    ready = after(attn_line, down_parts)
    qkv_first = chip_start(ready[:, :QKV], 0)
    mix_first = chip_start(ready[:, QKV:], 1)

    gate = (qkv_first, mix_first)
    qkv_own = chip_gather(*qkv_first, 0, gate)
    mix_own = chip_gather(*mix_first, 1, gate)
    qkv_weight = qkv_own + [across_rep(v, 1) for v in qkv_own]
    mix_weight = mix_own + [across_rep(v, 1) for v in mix_own]

    def line_up(n, earlier):
        chunk = pairs[n * per_chunk : (n + 1) * per_chunk].transpose(2, 0, 1, 3, 4)
        lined = exchange_blk(after(chunk, earlier)).transpose(1, 2, 0, 3, 4)
        return lined.reshape(per_chunk, 2 * cycle_size * rows_in, 4 * quarter)

    lines = [line_up(0, (attn_line, down_first))]

    expert_ids = jnp.arange(E, dtype=jnp.int32)
    dense = jnp.sum(
        jnp.where(
            routes[:, :, None] == expert_ids[None, None, :],
            gates.astype(F32)[:, :, None],
            F32(0.0),
        ),
        axis=1,
    ).astype(BF)
    sent = jnp.concatenate([tokens, jnp.pad(dense, ((0, 0), (0, 128 - E)))], axis=1)
    line = gather_blk(after(sent, (lines[0], qkv_first, mix_first))).reshape(group_rows, -1)
    group, group_gates = line[:, :D], line[:, D : D + E]

    for n in range(1, CHUNKS):
        lines.append(line_up(n, (line, lines[-1])))

    index = jnp.arange(group_rows, dtype=jnp.int32)
    begin = segment_begin(lengths[0], index)
    cosine, sine = rotation((index - begin).astype(F32))
    block = cycle_size * rows_in

    def attn_spots(turn):
        from_chip = chip ^ jnp.array(chip_order(turn), jnp.int32)
        from_rep = from_chip[None, :] * 2 + (core ^ jnp.arange(2, dtype=jnp.int32))[:, None]
        return (from_rep * block).reshape(-1)

    normed = rms_scale(group, attn_gain).astype(BF)
    up_parts, steps, gate = [], [], ()
    for n in range(CHUNKS):
        lined = after(lines[n], gate)
        first = [chip_start(lined[k], k % 2) for k in range(per_chunk)]
        parts = [chip_gather(*first[k], k % 2) for k in range(per_chunk)]
        up_parts.append([p.reshape(-1, 4 * quarter) for part in parts for p in part])
        steps += [first, parts]
        gate = (parts,)
        if n == 0:
            x = after(normed, (first,))
            qkv = project(attn_spots(0), block, x, cosine, sine, qkv_weight)
            attended = attend(qkv, begin, index)
            gate = (attended,)
    attended = after(attended, (steps[1],))
    span = D // (reps // 2)
    up_spots = (chip ^ jnp.arange(reps // 2, dtype=jnp.int32)) * span
    hidden, normed_two = mix(
        attn_spots(1), block, up_spots, span, attended, group, mix_weight, moe_gain
    )

    page_count = count // PAGE
    targets = place * page_count + jnp.arange(page_count, dtype=jnp.int32)
    table = page_table[0]
    logical = jnp.sum(
        jnp.where(
            table[None, :] == targets[:, None],
            jnp.arange(table.shape[0], dtype=jnp.int32)[None, :],
            0,
        ),
        axis=1,
    )
    first_row = logical * PAGE
    cache = qkv[:, QW:]
    kv_pages = jnp.stack(
        [lax.dynamic_slice_in_dim(cache, first_row[i], PAGE, 0) for i in range(page_count)]
    )

    other_two = across_rep(normed_two, 1)
    both_gates = jnp.concatenate([group_gates, across_rep(group_gates, 1)], axis=0)
    my_gates = lax.dynamic_slice_in_dim(both_gates, core * half_experts, half_experts, 1).astype(F32)
    chip_rows = 2 * rows_out
    whose = [chip ^ jnp.array(chip_order(n % 2), jnp.int32) for n in range(CHUNKS)]
    down_spots = [spots * chip_rows for spots in whose]
    if chip_rows % 16 != 0:
        for n, part in enumerate(down_parts):
            part = jnp.take(jnp.concatenate(part, axis=0), jnp.argsort(whose[n]), axis=0)
            part = part.transpose(1, 0, 2, 3)
            down_parts[n] = [part.reshape(1, part.shape[0], quarter, D)]

    orders, partial = [chip_order(k % 2) for k in range(per_chunk)], ()
    for n in range(CHUNKS):
        experts = slice(n * 2 * per_chunk, (n + 1) * 2 * per_chunk)
        weights = after(up_parts[n], partial)
        act = gate_up(orders, normed_two, other_two, my_gates[:, experts], weights)
        down = (down_spots[n], chip_rows, act, down_parts[n])
        if n + 1 < CHUNKS:
            partial = (down_project(*down, F32, addend=partial),)
        else:
            other = down_project(*down, BF, 1, 2, partial)
            came = across_rep(other, 1)
            mine = down_project(*down, F32, 0, 2, partial)

    def at(array, mask):
        return lax.dynamic_slice_in_dim(array, (place ^ mask) * count, count, 0).astype(F32)

    total = at(hidden, 0) + (at(mine, 0) + at(came, 0))
    for mask in range(1, cycle_size):
        part = (at(mine, mask) + at(came, mask)).astype(BF)
        total = total + across_blk(part, mask).astype(F32)
    return (total.astype(BF), kv_pages)


def solution(mesh):
    in_specs = (
        P(("rep", "blk"), None),
        P(("rep", "blk"), None),
        P(("rep", "blk"), None),
        P(None, ("rep", "blk"), None),
        P(None, ("rep", "blk"), None),
        P(),
        P(),
        P("rep", None),
        P("rep", None),
        P(("rep", "blk"), None),
        P(("rep", "blk"), None),
    )
    out_specs = (P(("rep", "blk"), None), P(("rep", "blk"), None, None))
    return jax.shard_map(body, mesh=mesh, in_specs=in_specs, out_specs=out_specs, check_vma=False)
```
